128 devices in a mesh: ctx: 32 (over y, z, x_lo), head: 4 (over x_hi, core).
Axes of the slice: x: 4 (x_hi: 2, x_lo: 2; x = x_hi * 2 + x_lo), y: 4, z: 4, core: 2. Of those that a mesh axis runs over, the one named last changes fastest.
Arguments:
- tokens: bfloat16 [16384, 1024], P('ctx'), may hold values from -24 to 24
- w_query: bfloat16 [1024, 1024], P(None, 'head'), may hold values from -0.1875 to 0.1875
- w_key: bfloat16 [1024, 1024], P(None, 'head'), may hold values from -0.1875 to 0.1875
- w_value: bfloat16 [1024, 1024], P(None, 'head'), may hold values from -0.1875 to 0.1875
- w_out: bfloat16 [1024, 1024], P('head'), may hold values from -0.1875 to 0.1875
- block_mask: int32 [128, 128], replicated, may hold values from 0 to 1, as said below
- block_order: int32 [128], replicated, may hold values from 0 to 127, each once
Outputs:
- mixed: bfloat16 [16384, 1024], P('ctx', 'head')
The draws below stay inside these ranges and needn't reach their ends.
Inputs may be any that keep to these rules, and one draw needn't show every extreme that they name: `block_mask`: entries are 0 or 1 and every diagonal entry is 1. `block_order`: each initial block index appears once.
All inputs are finite; a program needn't handle non-finite values.
Results may differ from the reference program's by a relative error of at most 0.013.
Values may be sent and summed in bfloat16 or wider, within the bound.
A program may use at most 256 MiB of HBM per device.

```python
import jax
import jax.numpy as jnp
from jax import lax

D = 1024
HEADS = 16
HEAD_DIM = 64
BLOCK = 128
TOKENS = 16384
NB = 128


def draw_tokens(key, part):
    key_base = jax.random.fold_in(key, 11)
    result = jnp.clip(jax.random.normal(key_base, (TOKENS, D), jnp.float32), -5.0, 5.0)
    return result.astype(jnp.bfloat16)


def draw_block_mask(key, part):
    key_width = jax.random.fold_in(key, 21)
    key_rates = jax.random.fold_in(key, 22)
    key_entry = jax.random.fold_in(key, 23)
    rows = jnp.arange(NB, dtype=jnp.int32)[:, None]
    cols = jnp.arange(NB, dtype=jnp.int32)[None, :]
    band_width = jax.random.randint(key_width, (NB, 1), 1, 5)
    band = jnp.abs(rows - cols) <= band_width
    row_rates = jnp.left_shift(1, jax.random.randint(key_rates, (NB, 1), 0, 5))
    entry_draw = jax.random.randint(key_entry, (NB, NB), 0, 256)
    cross = entry_draw < row_rates
    return jnp.where(band | cross, 1, 0).astype(jnp.int32)


def levels(rng, shape, shards, smallest, top_value):
    gain = 1.0
    for position, parts in shards:
        steps = jax.random.uniform(jax.random.fold_in(jax.random.fold_in(rng, 6), position), (parts,), jnp.float32, smallest / len(shards), top_value / len(shards))
        gain = gain * jnp.repeat(jnp.exp(steps), shape[position] // parts).reshape((-1,) + (1,) * (len(shape) - 1 - position))
    return gain


def normal_values(own_key, dims, scale, limit, cuts=(), kind=jnp.bfloat16):
    gain = levels(own_key, dims, cuts, -0.22, 0.18) if cuts else 1.0
    drawn = jax.random.normal(own_key, dims, jnp.float32) * scale * gain
    return jnp.minimum(jnp.maximum(drawn, -limit), limit).astype(kind)


def setup_inputs(seed: int = 0) -> dict:
    arg_keys = jax.random.split(jax.random.key(seed), 8)
    tokens = draw_tokens(jax.random.fold_in(arg_keys[7], 71), 0)
    w_query = normal_values(arg_keys[1], (D, D), D ** -0.5, 0.1875, ((1, 4),))
    w_key = normal_values(arg_keys[2], (D, D), D ** -0.5, 0.1875, ((1, 4),))
    w_value = normal_values(arg_keys[3], (D, D), D ** -0.5, 0.1875, ((1, 4),))
    w_out = normal_values(arg_keys[4], (D, D), D ** -0.5, 0.1875, ((0, 4),))
    block_mask = draw_block_mask(jax.random.fold_in(arg_keys[7], 71), 0)
    block_order = jax.random.permutation(arg_keys[6], NB).astype(jnp.int32)
    return {"tokens": tokens, "w_query": w_query, "w_key": w_key, "w_value": w_value, "w_out": w_out, "block_mask": block_mask, "block_order": block_order}


def reference(tokens, w_query, w_key, w_value, w_out, block_mask, block_order):
    query_proj = jnp.dot(tokens, w_query, preferred_element_type=jnp.float32).astype(jnp.bfloat16)
    key_proj = jnp.dot(tokens, w_key, preferred_element_type=jnp.float32).astype(jnp.bfloat16)
    value_proj = jnp.dot(tokens, w_value, preferred_element_type=jnp.float32).astype(jnp.bfloat16)
    query_heads = query_proj.reshape(TOKENS, HEADS, HEAD_DIM)
    key_heads = key_proj.reshape(TOKENS, HEADS, HEAD_DIM).astype(jnp.float32)
    value_heads = value_proj.reshape(TOKENS, HEADS, HEAD_DIM).astype(jnp.float32)
    ordered = jnp.take(jnp.take(block_mask, block_order, axis=0), block_order, axis=1)
    scale = HEAD_DIM ** -0.5

    def one_block(block_index):
        query_rows = lax.dynamic_slice_in_dim(query_heads, (block_index * BLOCK).astype(jnp.int32), BLOCK, 0).astype(jnp.float32)
        mask_row = lax.dynamic_index_in_dim(ordered, block_index.astype(jnp.int32), 0, keepdims=False)
        allowed = (jnp.repeat(mask_row, BLOCK) > 0)[None, None, :]
        scores = jnp.einsum("qhd,khd->hqk", query_rows, key_heads) * scale
        row_max = jnp.max(jnp.where(allowed, scores, -1e30), axis=2)
        probs = jnp.where(allowed, jnp.exp(scores - row_max[:, :, None]), 0.0)
        row_sum = jnp.sum(probs, axis=2)
        weighted = jnp.einsum("hqk,khd->qhd", probs.astype(jnp.bfloat16).astype(jnp.float32), value_heads)
        return (weighted / jnp.transpose(row_sum)[:, :, None]).astype(jnp.bfloat16)

    attended = lax.map(one_block, jnp.arange(NB, dtype=jnp.int32)).reshape(TOKENS, D)
    return jnp.dot(attended, w_out, preferred_element_type=jnp.float32).astype(jnp.bfloat16)
```

```python
import functools

import jax
import jax.numpy as jnp
from jax import lax
from jax.experimental import pallas as pl
from jax.experimental.pallas import tpu as pltpu
from jax.sharding import PartitionSpec as P

HEAD_DIM = 64
BLOCK = 128
NB = 128
ROWS = 512
NY, NZ = 4, 4
LIST_PAD = -1e30
MESH = pl.DeviceIdType.MESH
BF16 = jnp.bfloat16
F32 = jnp.float32


def place():
    ctx = lax.axis_index("ctx")
    head = lax.axis_index("head")
    return ctx // 8, (ctx // 2) % 4, ctx % 2, head // 2, head % 2


def ctx_of(y, z, x_lo):
    return (y * NZ + z) * 2 + x_lo


def project_kernel(tok_ref, wq_ref, wk_ref, wv_ref, mask_ref, order_row_ref, kv_ref, q_ref, lists_ref):
    tok = tok_ref[...]
    keys = jnp.dot(tok, wk_ref[...], preferred_element_type=F32).astype(BF16)
    vals = jnp.dot(tok, wv_ref[...], preferred_element_type=F32).astype(BF16)
    query = jnp.dot(tok, wq_ref[...], preferred_element_type=F32).astype(BF16)
    half = ROWS // 2
    for j in range(4):
        cols = slice(j * HEAD_DIM, (j + 1) * HEAD_DIM)
        kv_ref[j] = jnp.concatenate([keys[:, cols], vals[:, cols]], axis=1)
        q_ref[j] = jnp.concatenate([query[:half, cols], query[half:, cols]], axis=1)

    _, z, _, _, core = place()
    sub = lax.broadcasted_iota(jnp.int32, (NB, NB), 0)
    lane = lax.broadcasted_iota(jnp.int32, (NB, NB), 1)
    initial_of = (order_row_ref[...] == sub).astype(F32).astype(BF16)
    i16 = lax.broadcasted_iota(jnp.int32, (16, NB), 0)
    l16 = lax.broadcasted_iota(jnp.int32, (16, NB), 1)
    mine = ((i16 // 4 * NZ + z) * 2 + core) * 4 + i16 % 4
    row_pick = (l16 == mine).astype(F32).astype(BF16)
    rows_initial = lax.dot_general(
        row_pick, initial_of, (((1,), (1,)), ((), ())), preferred_element_type=F32
    ).astype(BF16)
    mask = mask_ref[...].astype(F32).astype(BF16)
    mask_rows = jnp.dot(rows_initial, mask, preferred_element_type=F32).astype(BF16)
    allowed = jnp.dot(mask_rows, initial_of, preferred_element_type=F32)
    before = (sub < lane).astype(F32).astype(BF16)
    rank = jnp.dot(allowed.astype(BF16), before, preferred_element_type=F32)
    rank = jnp.where(allowed > 0.5, rank, -1.0)
    lane_row = lax.broadcasted_iota(jnp.int32, (8, NB), 1).astype(F32).astype(BF16)
    sub_f = sub.astype(F32)
    for i in range(16):
        hot = (rank[i : i + 1, :] == sub_f).astype(F32).astype(BF16)
        got = lax.dot_general(lane_row, hot, (((1,), (1,)), ((), ())), preferred_element_type=F32)
        lists_ref[i : i + 1, :] = got[0:1, :].astype(jnp.int32)
    count = jnp.sum(allowed, axis=1, keepdims=True)
    lists_ref[16:32, :] = jnp.broadcast_to(count, (16, NB)).astype(jnp.int32)


def project(tokens, w_query, w_key, w_value, block_mask, order_row):
    whole = pl.BlockSpec(memory_space=pltpu.VMEM)
    return pl.pallas_call(
        project_kernel,
        out_shape=(
            jax.ShapeDtypeStruct((4, ROWS, 128), BF16),
            jax.ShapeDtypeStruct((4, ROWS // 2, 128), BF16),
            jax.ShapeDtypeStruct((32, NB), jnp.int32),
        ),
        in_specs=[whole] * 6,
        out_specs=(whole, whole, whole),
        name="project",
    )(tokens, w_query, w_key, w_value, block_mask, order_row)


def exchange_kernel(kv_ref, q_ref, w_ref, kv_all, q_all, w_all, a_send, a_recv, q_send, q_recv, w_send, w_recv,
                    z_send, z_recv, c_send, c_recv):
    y, z, x_lo, x_hi, core = place()
    me_ctx = ctx_of(y, z, x_lo)
    me_head = x_hi * 2 + core
    swap_head = x_hi * 2 + x_lo
    stays = x_lo == core
    up = (ctx_of(y, (z + 1) % NZ, x_lo), me_head)
    down = (ctx_of(y, (z + 3) % NZ, x_lo), me_head)
    twin = (me_ctx, x_hi * 2 + 1 - core)
    head_peers = [(me_ctx, (me_head + k) % 4) for k in range(1, 4)]
    a_to = [(ctx_of((y + d) % NY, z, core), swap_head) for d in range(4)]

    barrier = pltpu.get_barrier_semaphore()
    for peer in [up, down, *head_peers, *a_to[1:]]:
        pl.semaphore_signal(barrier, inc=1, device_id=peer, device_id_type=MESH)

    @pl.when(jnp.logical_not(stays))
    def _():
        pl.semaphore_signal(barrier, inc=1, device_id=a_to[0], device_id_type=MESH)

    pl.semaphore_wait(barrier, 8 + (x_lo + core) % 2)

    def remote(src, dst, send_sem, recv_sem, device):
        return pltpu.make_async_remote_copy(
            src_ref=src, dst_ref=dst, send_sem=send_sem, recv_sem=recv_sem, device_id=device, device_id_type=MESH
        )

    sent = []

    def send(src, dst, send_sem, recv_sem, device):
        copy = remote(src, dst, send_sem, recv_sem, device)
        copy.start()
        sent.append(copy)

    def arrived(dst, send_sem, recv_sem, device):
        remote(dst, dst, send_sem, recv_sem, device).wait_recv()

    own = y % NY
    kv_here = remote(kv_ref.at[own], kv_all.at[me_ctx], a_send.at[0], a_recv.at[0], a_to[0])
    q_here = remote(q_ref.at[own], q_all.at[y], q_send.at[0], q_recv.at[0], a_to[0])
    kv_local = pltpu.make_async_copy(kv_ref.at[own], kv_all.at[me_ctx], a_recv.at[0])
    q_local = pltpu.make_async_copy(q_ref.at[own], q_all.at[y], q_recv.at[0])

    @pl.when(stays)
    def _():
        kv_local.start()
        q_local.start()

    @pl.when(jnp.logical_not(stays))
    def _():
        kv_here.start()
        q_here.start()

    order = (1, 3, 2)
    for d in order:
        send(kv_ref.at[(y + d) % NY], kv_all.at[me_ctx], a_send.at[d], a_recv.at[d], a_to[d])
    for d in order:
        send(q_ref.at[(y + d) % NY], q_all.at[y], q_send.at[d], q_recv.at[d], a_to[d])
    for k in range(1, 4):
        to = (me_head + k) % 4
        send(w_ref.at[:, pl.ds(pl.multiple_of(to * 256, 256), 256)], w_all.at[me_head], w_send.at[k - 1], w_recv.at[k - 1],
             head_peers[k - 1])
    w_local = pltpu.make_async_copy(
        w_ref.at[:, pl.ds(pl.multiple_of(me_head * 256, 256), 256)], w_all.at[me_head], w_recv.at[3]
    )
    w_local.start()

    def chunk(d, dz):
        return kv_all.at[ctx_of((y + NY - d) % NY, (z + NZ + dz) % NZ, core)]

    for d in (0, 1, 3, 2):
        if d == 0:
            @pl.when(stays)
            def _():
                kv_local.wait()

            @pl.when(jnp.logical_not(stays))
            def _():
                kv_here.wait_recv()
        else:
            arrived(chunk(d, 0), a_send.at[d], a_recv.at[d], a_to[d])
        send(chunk(d, 0), chunk(d, 0), z_send.at[d], z_recv.at[d], up)
        send(chunk(d, 0), chunk(d, 0), z_send.at[4 + d], z_recv.at[4 + d], down)
        send(chunk(d, 0), chunk(d, 0), c_send.at[d], c_recv.at[d], twin)
    for d in (0, 1, 3, 2):
        below, above = chunk(d, -1), chunk(d, 1)
        arrived(below, z_send.at[d], z_recv.at[d], up)
        if d in (0, 1):
            send(below, below, z_send.at[8 + d], z_recv.at[8 + d], up)
        send(below, below, c_send.at[4 + d], c_recv.at[4 + d], twin)
        arrived(above, z_send.at[4 + d], z_recv.at[4 + d], down)
        if d in (2, 3):
            send(above, above, z_send.at[8 + d], z_recv.at[8 + d], down)
        send(above, above, c_send.at[8 + d], c_recv.at[8 + d], twin)
    for d in (0, 1, 3, 2):
        far = chunk(d, 2)
        arrived(far, z_send.at[8 + d], z_recv.at[8 + d], up)
        send(far, far, c_send.at[12 + d], c_recv.at[12 + d], twin)

    def twin_chunk(d, dz):
        return kv_all.at[ctx_of((y + NY - d) % NY, (z + NZ + dz) % NZ, 1 - core)]

    for place_of, dz in ((0, 0), (4, -1), (8, 1), (12, 2)):
        for d in (0, 1, 3, 2):
            arrived(twin_chunk(d, dz), c_send.at[place_of + d], c_recv.at[place_of + d], twin)

    @pl.when(stays)
    def _():
        q_local.wait()

    @pl.when(jnp.logical_not(stays))
    def _():
        q_here.wait_recv()
        kv_here.wait_send()
        q_here.wait_send()

    for d in order:
        arrived(q_all.at[(y + NY - d) % NY], q_send.at[d], q_recv.at[d], a_to[d])
    for k in range(1, 4):
        arrived(w_all.at[(me_head + 4 - k) % 4], w_send.at[k - 1], w_recv.at[k - 1], head_peers[k - 1])
    w_local.wait()
    for copy in sent:
        copy.wait_send()


def exchange(kv, query, w_out):
    anywhere = pl.BlockSpec(memory_space=pl.ANY)
    dma = pltpu.SemaphoreType.DMA
    return pl.pallas_call(
        exchange_kernel,
        out_shape=(
            jax.ShapeDtypeStruct((32, ROWS, 128), BF16),
            jax.ShapeDtypeStruct((4, ROWS // 2, 128), BF16),
            jax.ShapeDtypeStruct((4, 256, 256), BF16),
        ),
        in_specs=[anywhere] * 3,
        out_specs=(anywhere,) * 3,
        scratch_shapes=[
            dma((4,)), dma((4,)), dma((4,)), dma((4,)), dma((4,)), dma((4,)),
            dma((12,)), dma((12,)), dma((16,)), dma((16,)),
        ],
        compiler_params=pltpu.CompilerParams(collective_id=0, has_side_effects=True),
        name="exchange",
    )(kv, query, w_out)


UNROLL = 4
EXP2_SCALE = (HEAD_DIM ** -0.5) * 1.4426950408889634


def attend_kernel(lists, q_ref, kv_ref, out_ref, qz, scores):
    lanes = lax.broadcasted_iota(jnp.int32, (BLOCK, 128), 1)
    nt = (((1,), (1,)), ((), ()))

    def owner(step, _):
        for b in range(4):
            row0 = (b % 2) * BLOCK
            q = q_ref[step, row0 : row0 + BLOCK, :]
            if b // 2:
                q = jnp.concatenate([q[:, HEAD_DIM:], q[:, :HEAD_DIM]], axis=1)
            qz[b] = jnp.where(lanes < HEAD_DIM, q, jnp.zeros_like(q))
        for b in range(4):
            i = step * 4 + b
            n = lists[16 + i, 0]
            groups = (n + UNROLL - 1) // UNROLL
            q = qz[b]

            def keys_at(k):
                start = pl.multiple_of(lists[i, k] * BLOCK, BLOCK)
                return kv_ref[pl.ds(start, BLOCK), :]

            def first(g, top):
                for u in range(UNROLL):
                    k = g * UNROLL + u
                    bias = jnp.where(k < n, 0.0, LIST_PAD).astype(F32)
                    s = lax.dot_general(q, keys_at(k), nt, preferred_element_type=F32) + bias
                    scores[k] = s
                    top = jnp.maximum(top, s)
                return top

            top = lax.fori_loop(0, groups, first, jnp.full((BLOCK, BLOCK), -3e38, F32))
            top = jnp.max(top, axis=1, keepdims=True)

            def second(g, carry):
                total, acc = carry
                probs, blocks = [], []
                for u in range(UNROLL):
                    k = g * UNROLL + u
                    p = jnp.exp2((scores[k] - top) * EXP2_SCALE)
                    total = total + p
                    probs.append(p.astype(BF16))
                    blocks.append(keys_at(k))
                acc = acc + jnp.dot(
                    jnp.concatenate(probs, axis=1), jnp.concatenate(blocks, axis=0), preferred_element_type=F32
                )
                return total, acc

            zero = jnp.zeros((BLOCK, 128), F32)
            total, acc = lax.fori_loop(0, groups, second, (zero, zero))
            denom = jnp.sum(total, axis=1, keepdims=True)
            row0, col0 = (b % 2) * BLOCK, (b // 2) * HEAD_DIM
            out_ref[step, row0 : row0 + BLOCK, col0 : col0 + HEAD_DIM] = (acc[:, HEAD_DIM:] / denom).astype(BF16)
        return 0

    lax.fori_loop(0, 4, owner, 0)


def attend(lists, query, kv):
    whole = pl.BlockSpec(memory_space=pltpu.VMEM)
    return pl.pallas_call(
        attend_kernel,
        out_shape=jax.ShapeDtypeStruct((4, ROWS // 2, 128), BF16),
        grid_spec=pltpu.PrefetchScalarGridSpec(
            num_scalar_prefetch=1,
            grid=(),
            in_specs=[whole, whole],
            out_specs=whole,
            scratch_shapes=[pltpu.VMEM((4, BLOCK, 128), BF16), pltpu.VMEM((NB, BLOCK, BLOCK), F32)],
        ),
        compiler_params=pltpu.CompilerParams(vmem_limit_bytes=32 << 20),
        name="attend",
    )(lists, query, kv)


def return_kernel(att_ref, all_ref, send_sems, recv_sems, c_send, c_recv):
    y, z, x_lo, x_hi, core = place()
    me_ctx = ctx_of(y, z, x_lo)
    stays = x_lo == core
    twin = (me_ctx, x_hi * 2 + 1 - core)
    me_global = (x_hi * 2 + x_lo) * 4 + y
    near = [(ctx_of((y + d) % NY, z, core), x_hi * 2 + x_lo) for d in range(4)]
    cross = [(ctx_of((y + d) % NY, z, core), (1 - x_hi) * 2 + x_lo) for d in range(4)]

    barrier = pltpu.get_barrier_semaphore()
    for peer in [twin, *cross, *near[1:]]:
        pl.semaphore_signal(barrier, inc=1, device_id=peer, device_id_type=MESH)

    @pl.when(jnp.logical_not(stays))
    def _():
        pl.semaphore_signal(barrier, inc=1, device_id=near[0], device_id_type=MESH)

    pl.semaphore_wait(barrier, 8 + (x_lo + core) % 2)

    def remote(src, dst, send_sem, recv_sem, device):
        return pltpu.make_async_remote_copy(
            src_ref=src, dst_ref=dst, send_sem=send_sem, recv_sem=recv_sem, device_id=device, device_id_type=MESH
        )

    sent = []

    def send(src, dst, send_sem, recv_sem, device):
        copy = remote(src, dst, send_sem, recv_sem, device)
        copy.start()
        sent.append(copy)

    for d in range(4):
        send(att_ref.at[(y + d) % NY], all_ref.at[me_global], send_sems.at[4 + d], recv_sems.at[4 + d], cross[d])
    here = remote(att_ref.at[y], all_ref.at[me_global], send_sems.at[0], recv_sems.at[0], near[0])
    local = pltpu.make_async_copy(att_ref.at[y], all_ref.at[me_global], recv_sems.at[0])

    @pl.when(stays)
    def _():
        local.start()

    @pl.when(jnp.logical_not(stays))
    def _():
        here.start()

    for d in range(1, 4):
        send(att_ref.at[(y + d) % NY], all_ref.at[me_global], send_sems.at[d], recv_sems.at[d], near[d])

    def of(source_hi, source_lo, d):
        return all_ref.at[(source_hi * 2 + source_lo) * 4 + (y + NY - d) % NY]

    for d in (0, 1, 3, 2):
        got = of(x_hi, core, d)
        if d == 0:
            @pl.when(stays)
            def _():
                local.wait()

            @pl.when(jnp.logical_not(stays))
            def _():
                here.wait_recv()
        else:
            remote(got, got, send_sems.at[d], recv_sems.at[d], near[d]).wait_recv()
        send(got, got, c_send.at[d], c_recv.at[d], twin)
    for d in (0, 1, 3, 2):
        got = of(1 - x_hi, core, d)
        remote(got, got, send_sems.at[4 + d], recv_sems.at[4 + d], cross[d]).wait_recv()
        send(got, got, c_send.at[4 + d], c_recv.at[4 + d], twin)
    for d in (0, 1, 3, 2):
        got = of(x_hi, 1 - core, d)
        remote(got, got, c_send.at[d], c_recv.at[d], twin).wait_recv()
    for d in (0, 1, 3, 2):
        got = of(1 - x_hi, 1 - core, d)
        remote(got, got, c_send.at[4 + d], c_recv.at[4 + d], twin).wait_recv()

    @pl.when(jnp.logical_not(stays))
    def _():
        here.wait_send()

    for copy in sent:
        copy.wait_send()


def give_back(attended):
    anywhere = pl.BlockSpec(memory_space=pl.ANY)
    dma = pltpu.SemaphoreType.DMA
    return pl.pallas_call(
        return_kernel,
        out_shape=jax.ShapeDtypeStruct((16, ROWS // 2, 128), BF16),
        in_specs=[anywhere],
        out_specs=anywhere,
        scratch_shapes=[dma((8,)), dma((8,)), dma((8,)), dma((8,))],
        compiler_params=pltpu.CompilerParams(collective_id=1, has_side_effects=True),
        name="give_back",
    )(attended)


def mix_kernel(att_ref, w_ref, out_ref):
    w = w_ref[...]
    half = ROWS // 2
    for side in range(2):
        cols = slice(side * HEAD_DIM, (side + 1) * HEAD_DIM)
        a = jnp.concatenate([att_ref[g][:, cols] for g in range(16)], axis=1)
        out_ref[side * half : (side + 1) * half, :] = jnp.dot(a, w, preferred_element_type=F32).astype(BF16)


def mix(attended, w_cols):
    whole = pl.BlockSpec(memory_space=pltpu.VMEM)
    return pl.pallas_call(
        mix_kernel,
        out_shape=jax.ShapeDtypeStruct((ROWS, 256), BF16),
        in_specs=[whole, whole],
        out_specs=whole,
        name="mix",
    )(attended, w_cols)


def body(tokens, w_query, w_key, w_value, w_out, block_mask, block_order):
    kv, query, lists = project(tokens, w_query, w_key, w_value, block_mask, block_order.reshape(1, NB))
    kv_all, q_all, w_all = exchange(kv, query, w_out)
    attended = attend(lists, q_all, kv_all.reshape(32 * ROWS, 128))
    everything = give_back(attended)
    return mix(everything, w_all.reshape(1024, 256))


def solution(mesh):
    placed = (P("ctx", None), P(None, "head"), P(None, "head"), P(None, "head"), P("head", None), P(), P())
    return jax.shard_map(body, mesh=mesh, in_specs=placed, out_specs=P("ctx", "head"), check_vma=False)
```

```python
import functools

import jax
import jax.numpy as jnp
from jax import lax
from jax.experimental import pallas as pl
from jax.experimental.pallas import tpu as pltpu
from jax.sharding import PartitionSpec as P

HEAD_DIM = 64
BLOCK = 128
NB = 128
ROWS = 512
NY, NZ = 4, 4
LIST_PAD = -1e30
MESH = pl.DeviceIdType.MESH
BF16 = jnp.bfloat16
F32 = jnp.float32


def place():
    ctx = lax.axis_index("ctx")
    head = lax.axis_index("head")
    return ctx // 8, (ctx // 2) % 4, ctx % 2, head // 2, head % 2


def ctx_of(y, z, x_lo):
    return (y * NZ + z) * 2 + x_lo


def write_lists(mask, order_row, z, core, lists_ref):
    sub = lax.broadcasted_iota(jnp.int32, (NB, NB), 0)
    lane = lax.broadcasted_iota(jnp.int32, (NB, NB), 1)
    nt = (((1,), (1,)), ((), ()))

    def as_bf16(condition):
        return condition.astype(F32).astype(BF16)

    initial_of = as_bf16(order_row == sub)
    mine = ((sub // 4 * NZ + z) * 2 + core) * 4 + sub % 4
    row_pick = as_bf16(jnp.logical_and(lane == mine, sub < 16))
    rows_initial = lax.dot_general(row_pick, initial_of, nt, preferred_element_type=F32).astype(BF16)
    mask_rows = jnp.dot(rows_initial, mask.astype(F32).astype(BF16), preferred_element_type=F32).astype(BF16)
    allowed = jnp.dot(mask_rows, initial_of, preferred_element_type=F32)
    rank = jnp.dot(allowed.astype(BF16), as_bf16(sub < lane), preferred_element_type=F32)
    rank = jnp.where(allowed > 0.5, rank, -1.0)
    sub_f = sub.astype(F32)
    lane_row = lax.broadcasted_iota(jnp.int32, (8, NB), 1).astype(F32).astype(BF16)
    for i in range(16):
        hot = as_bf16(rank[i : i + 1, :] == sub_f)
        got = lax.dot_general(lane_row, hot, nt, preferred_element_type=F32)
        lists_ref[i : i + 1, :] = got[0:1, :].astype(jnp.int32)
    ones = jnp.ones((8, NB), BF16)
    count = lax.dot_general(ones, allowed.astype(BF16), nt, preferred_element_type=F32)
    steps = jnp.floor((count + 1.0) * 0.5)
    total = jnp.sum(steps, axis=1, keepdims=True)
    counts = jnp.where(lane[0:8] == 32, total, count).astype(jnp.int32)
    lists_ref[16:32, :] = jnp.zeros((16, NB), jnp.int32)
    lists_ref[17:18, :] = counts[0:1]


def exchange_kernel(tok_hbm, wq_hbm, wk_hbm, wv_hbm, w_ref, mask_hbm, order_hbm, kv_all, q_all, w_all, lists_ref,
                    tok_ref, wq_ref, wk_ref, wv_ref, mask_ref, order_ref, kv_ref, q_ref, in_sems,
                    a_send, a_recv, q_send, q_recv, w_send, w_recv, z_send, z_recv, c_send, c_recv):
    loads = [
        pltpu.make_async_copy(src, dst, in_sems.at[n])
        for n, (src, dst) in enumerate(
            [(wk_hbm, wk_ref), (tok_hbm, tok_ref), (wv_hbm, wv_ref), (wq_hbm, wq_ref), (mask_hbm, mask_ref), (order_hbm, order_ref)]
        )
    ]
    for load in loads:
        load.start()
    y, z, x_lo, x_hi, core = place()
    me_ctx = ctx_of(y, z, x_lo)
    me_head = x_hi * 2 + core
    swap_head = x_hi * 2 + x_lo
    stays = x_lo == core
    up = (ctx_of(y, (z + 1) % NZ, x_lo), me_head)
    down = (ctx_of(y, (z + 3) % NZ, x_lo), me_head)
    twin = (me_ctx, x_hi * 2 + 1 - core)
    head_peers = [(me_ctx, (me_head + k) % 4) for k in range(1, 4)]
    a_to = [(ctx_of((y + d) % NY, z, core), swap_head) for d in range(4)]

    barrier = pltpu.get_barrier_semaphore()
    for peer in [up, down, *head_peers, *a_to[1:]]:
        pl.semaphore_signal(barrier, inc=1, device_id=peer, device_id_type=MESH)

    @pl.when(jnp.logical_not(stays))
    def _():
        pl.semaphore_signal(barrier, inc=1, device_id=a_to[0], device_id_type=MESH)

    half = ROWS // 2
    columns = [slice(j * HEAD_DIM, (j + 1) * HEAD_DIM) for j in range(4)]
    loads[0].wait()
    loads[1].wait()
    tok = tok_ref[...]
    keys = jnp.dot(tok, wk_ref[...], preferred_element_type=F32).astype(BF16)
    loads[2].wait()
    vals = jnp.dot(tok, wv_ref[...], preferred_element_type=F32).astype(BF16)
    for j in range(4):
        kv_ref[j] = jnp.concatenate([keys[:, columns[j]], vals[:, columns[j]]], axis=1)

    pl.semaphore_wait(barrier, 8 + (x_lo + core) % 2)

    def remote(src, dst, send_sem, recv_sem, device):
        return pltpu.make_async_remote_copy(
            src_ref=src, dst_ref=dst, send_sem=send_sem, recv_sem=recv_sem, device_id=device, device_id_type=MESH
        )

    sent = []

    def send(src, dst, send_sem, recv_sem, device):
        copy = remote(src, dst, send_sem, recv_sem, device)
        copy.start()
        sent.append(copy)

    def arrived(dst, send_sem, recv_sem, device):
        remote(dst, dst, send_sem, recv_sem, device).wait_recv()

    own = y % NY
    kv_here = remote(kv_ref.at[own], kv_all.at[me_ctx], a_send.at[0], a_recv.at[0], a_to[0])
    q_here = remote(q_ref.at[own], q_all.at[y], q_send.at[0], q_recv.at[0], a_to[0])
    kv_local = pltpu.make_async_copy(kv_ref.at[own], kv_all.at[me_ctx], a_recv.at[0])
    q_local = pltpu.make_async_copy(q_ref.at[own], q_all.at[y], q_recv.at[0])

    @pl.when(stays)
    def _():
        kv_local.start()

    @pl.when(jnp.logical_not(stays))
    def _():
        kv_here.start()

    order = (1, 3, 2)
    for d in order:
        send(kv_ref.at[(y + d) % NY], kv_all.at[me_ctx], a_send.at[d], a_recv.at[d], a_to[d])
    loads[3].wait()
    query = jnp.dot(tok, wq_ref[...], preferred_element_type=F32).astype(BF16)
    for j in range(4):
        q_ref[j] = jnp.concatenate([query[:half, columns[j]], query[half:, columns[j]]], axis=1)

    @pl.when(stays)
    def _():
        q_local.start()

    @pl.when(jnp.logical_not(stays))
    def _():
        q_here.start()

    for d in order:
        send(q_ref.at[(y + d) % NY], q_all.at[y], q_send.at[d], q_recv.at[d], a_to[d])
    for k in range(1, 4):
        to = (me_head + k) % 4
        send(w_ref.at[:, pl.ds(pl.multiple_of(to * 256, 256), 256)], w_all.at[me_head], w_send.at[k - 1], w_recv.at[k - 1],
             head_peers[k - 1])
    w_local = pltpu.make_async_copy(
        w_ref.at[:, pl.ds(pl.multiple_of(me_head * 256, 256), 256)], w_all.at[me_head], w_recv.at[3]
    )
    w_local.start()

    def chunk(d, dz):
        return kv_all.at[ctx_of((y + NY - d) % NY, (z + NZ + dz) % NZ, core)]

    for d in (0, 1, 3, 2):
        if d == 0:
            @pl.when(stays)
            def _():
                kv_local.wait()

            @pl.when(jnp.logical_not(stays))
            def _():
                kv_here.wait_recv()
        else:
            arrived(chunk(d, 0), a_send.at[d], a_recv.at[d], a_to[d])
        send(chunk(d, 0), chunk(d, 0), z_send.at[d], z_recv.at[d], up)
        send(chunk(d, 0), chunk(d, 0), z_send.at[4 + d], z_recv.at[4 + d], down)
        send(chunk(d, 0), chunk(d, 0), c_send.at[d], c_recv.at[d], twin)
        if d == 0:
            loads[4].wait()
            loads[5].wait()
            write_lists(mask_ref[...], order_ref[...], z, core, lists_ref)
    for d in (0, 1, 3, 2):
        below, above = chunk(d, -1), chunk(d, 1)
        arrived(below, z_send.at[d], z_recv.at[d], up)
        if d in (0, 1):
            send(below, below, z_send.at[8 + d], z_recv.at[8 + d], up)
        send(below, below, c_send.at[4 + d], c_recv.at[4 + d], twin)
        arrived(above, z_send.at[4 + d], z_recv.at[4 + d], down)
        if d in (2, 3):
            send(above, above, z_send.at[8 + d], z_recv.at[8 + d], down)
        send(above, above, c_send.at[8 + d], c_recv.at[8 + d], twin)
    for d in (0, 1, 3, 2):
        far = chunk(d, 2)
        arrived(far, z_send.at[8 + d], z_recv.at[8 + d], up)
        send(far, far, c_send.at[12 + d], c_recv.at[12 + d], twin)

    def twin_chunk(d, dz):
        return kv_all.at[ctx_of((y + NY - d) % NY, (z + NZ + dz) % NZ, 1 - core)]

    for place_of, dz in ((0, 0), (4, -1), (8, 1), (12, 2)):
        for d in (0, 1, 3, 2):
            arrived(twin_chunk(d, dz), c_send.at[place_of + d], c_recv.at[place_of + d], twin)

    @pl.when(stays)
    def _():
        q_local.wait()

    @pl.when(jnp.logical_not(stays))
    def _():
        q_here.wait_recv()
        kv_here.wait_send()
        q_here.wait_send()

    for d in order:
        arrived(q_all.at[(y + NY - d) % NY], q_send.at[d], q_recv.at[d], a_to[d])
    for k in range(1, 4):
        arrived(w_all.at[(me_head + 4 - k) % 4], w_send.at[k - 1], w_recv.at[k - 1], head_peers[k - 1])
    w_local.wait()
    for copy in sent:
        copy.wait_send()


def exchange(tokens, w_query, w_key, w_value, w_out, block_mask, order_row):
    in_hbm = pl.BlockSpec(memory_space=pltpu.HBM)
    operands = [tokens, w_query, w_key, w_value, w_out, block_mask, order_row]
    operands = [pltpu.with_memory_space_constraint(a, pltpu.HBM) for a in operands]
    anywhere = pl.BlockSpec(memory_space=pl.ANY)
    dma = pltpu.SemaphoreType.DMA
    vmem = pltpu.VMEM
    return pl.pallas_call(
        exchange_kernel,
        out_shape=(
            jax.ShapeDtypeStruct((32, ROWS, 128), BF16),
            jax.ShapeDtypeStruct((4, ROWS // 2, 128), BF16),
            jax.ShapeDtypeStruct((4, 256, 256), BF16),
            jax.ShapeDtypeStruct((32, NB), jnp.int32),
        ),
        in_specs=[in_hbm] * 7,
        out_specs=(anywhere,) * 3 + (pl.BlockSpec(memory_space=vmem),),
        scratch_shapes=[
            vmem((ROWS, 1024), BF16), vmem((1024, 256), BF16), vmem((1024, 256), BF16), vmem((1024, 256), BF16),
            vmem((NB, NB), jnp.int32), vmem((1, NB), jnp.int32), vmem((4, ROWS, 128), BF16), vmem((4, ROWS // 2, 128), BF16),
            dma((6,)),
            dma((4,)), dma((4,)), dma((4,)), dma((4,)), dma((4,)), dma((4,)),
            dma((12,)), dma((12,)), dma((16,)), dma((16,)),
        ],
        compiler_params=pltpu.CompilerParams(collective_id=0, has_side_effects=True, vmem_limit_bytes=16 << 20),
        name="exchange",
    )(*operands)


UNROLL = 4
EXP2_SCALE = (HEAD_DIM ** -0.5) * 1.4426950408889634
SMALLEST, LARGEST = 1e-20, 1e30
NT = (((1,), (1,)), ((), ()))


def query_place(i):
    b = i % 4
    return i // 4, slice(b % 2 * BLOCK, (b % 2 + 1) * BLOCK), slice(b // 2 * HEAD_DIM, (b // 2 + 1) * HEAD_DIM)


def attend_kernel(lists, q_ref, kv_ref, out_ref, qz, acc, ones_v, sbuf, scores):
    left = lax.broadcasted_iota(jnp.int32, (BLOCK, 128), 1) < HEAD_DIM
    zero = jnp.zeros((BLOCK, 128), F32)
    for i in range(16):
        y, rows, cols = query_place(i)
        q = q_ref[y, rows, :]
        if cols.start:
            q = jnp.concatenate([q[:, HEAD_DIM:], q[:, :HEAD_DIM]], axis=1)
        qz[i] = jnp.where(left, q, jnp.zeros_like(q))
        acc[i] = zero
    qz[16] = jnp.zeros((BLOCK, 128), BF16)
    acc[16] = zero

    def fill(t, _):
        part = pl.ds(pl.multiple_of(t * 1024, 1024), 1024)
        lanes = lax.broadcasted_iota(jnp.int32, (1024, 128), 1)
        ones_v[part, :] = jnp.where(lanes < HEAD_DIM, jnp.ones((1024, 128), BF16), kv_ref[part, :])
        return 0

    lax.fori_loop(0, 16, fill, 0)
    second = lax.broadcasted_iota(jnp.int32, (1, 2 * BLOCK), 1) >= BLOCK

    def rows_at(i, k):
        return pl.ds(pl.multiple_of(lists[i, jnp.minimum(k, NB - 1)] * BLOCK, BLOCK), BLOCK)

    def advance(i, k):
        done = k + 2 >= lists[17, i]
        return jnp.minimum(jnp.where(done, i + 1, i), 16), jnp.where(done, 0, k + 2)

    def score(slot, i, k):
        for u in range(UNROLL):
            keys = jnp.concatenate([kv_ref[rows_at(i, k), :], kv_ref[rows_at(i, k + 1), :]], axis=0)
            sbuf[slot, u] = lax.dot_general(qz[i], keys, NT, preferred_element_type=F32)
            i, k = advance(i, k)
        return i, k

    def weigh(slot, i, k):
        for u in range(UNROLL):
            bias = jnp.where(k + 1 < lists[17, i], 0.0, LIST_PAD).astype(F32)
            vals = jnp.concatenate([ones_v[rows_at(i, k), :], ones_v[rows_at(i, k + 1), :]], axis=0)
            p = jnp.exp2(sbuf[slot, u] * EXP2_SCALE + jnp.where(second, bias, 0.0)).astype(BF16)
            acc[i] += jnp.dot(p, vals, preferred_element_type=F32)
            i, k = advance(i, k)

    start = jnp.int32(0)
    i1, k1 = score(0, start, start)

    def step(_, carry):
        i, k, i1, k1 = carry
        i2, k2 = score(1, i1, k1)
        weigh(0, i, k)
        i3, k3 = score(0, i2, k2)
        weigh(1, i1, k1)
        return i2, k2, i3, k3

    lax.fori_loop(0, (lists[17, 32] + 2 * UNROLL - 1) // (2 * UNROLL), step, (start, start, i1, k1))

    fine = jnp.full((BLOCK, HEAD_DIM), 1.0, F32)
    for i in range(16):
        y, rows, cols = query_place(i)
        denom = acc[i][:, :HEAD_DIM]
        within = jnp.logical_and(denom >= SMALLEST, denom <= LARGEST)
        fine = jnp.where(within, fine, 0.0)
        out_ref[y, rows, cols] = (acc[i][:, HEAD_DIM:] / denom).astype(BF16)

    @pl.when(jnp.min(fine) < 0.5)
    def _():
        for i in range(16):
            y, rows, cols = query_place(i)
            n = lists[17, i]

            def first(k, top):
                s = lax.dot_general(qz[i], kv_ref[rows_at(i, k), :], NT, preferred_element_type=F32)
                scores[k] = s
                return jnp.maximum(top, s)

            top = lax.fori_loop(0, n, first, jnp.full((BLOCK, BLOCK), -3e38, F32))
            top = jnp.max(top, axis=1, keepdims=True)

            def then(k, carry):
                total, weighted = carry
                p = jnp.exp2((scores[k] - top) * EXP2_SCALE)
                return total + p, weighted + jnp.dot(
                    p.astype(BF16), kv_ref[rows_at(i, k), :], preferred_element_type=F32
                )

            total, weighted = lax.fori_loop(0, n, then, (zero, zero))
            denom = jnp.sum(total, axis=1, keepdims=True)
            out_ref[y, rows, cols] = (weighted[:, HEAD_DIM:] / denom).astype(BF16)


def attend(lists, query, kv):
    whole = pl.BlockSpec(memory_space=pltpu.VMEM)
    vmem = pltpu.VMEM
    return pl.pallas_call(
        attend_kernel,
        out_shape=jax.ShapeDtypeStruct((4, ROWS // 2, 128), BF16),
        grid_spec=pltpu.PrefetchScalarGridSpec(
            num_scalar_prefetch=1,
            grid=(),
            in_specs=[whole, whole],
            out_specs=whole,
            scratch_shapes=[
                vmem((17, BLOCK, 128), BF16),
                vmem((17, BLOCK, 128), F32),
                vmem((32 * ROWS, 128), BF16),
                vmem((2, UNROLL, BLOCK, 2 * BLOCK), F32),
                vmem((NB, BLOCK, BLOCK), F32),
            ],
        ),
        compiler_params=pltpu.CompilerParams(vmem_limit_bytes=28 << 20),
        name="attend",
    )(lists, query, kv)


def return_kernel(att_ref, all_ref, send_sems, recv_sems, c_send, c_recv):
    y, z, x_lo, x_hi, core = place()
    me_ctx = ctx_of(y, z, x_lo)
    stays = x_lo == core
    twin = (me_ctx, x_hi * 2 + 1 - core)
    me_global = (x_hi * 2 + x_lo) * 4 + y
    near = [(ctx_of((y + d) % NY, z, core), x_hi * 2 + x_lo) for d in range(4)]
    cross = [(ctx_of((y + d) % NY, z, core), (1 - x_hi) * 2 + x_lo) for d in range(4)]

    barrier = pltpu.get_barrier_semaphore()
    for peer in [twin, *cross, *near[1:]]:
        pl.semaphore_signal(barrier, inc=1, device_id=peer, device_id_type=MESH)

    @pl.when(jnp.logical_not(stays))
    def _():
        pl.semaphore_signal(barrier, inc=1, device_id=near[0], device_id_type=MESH)

    pl.semaphore_wait(barrier, 8 + (x_lo + core) % 2)

    def remote(src, dst, send_sem, recv_sem, device):
        return pltpu.make_async_remote_copy(
            src_ref=src, dst_ref=dst, send_sem=send_sem, recv_sem=recv_sem, device_id=device, device_id_type=MESH
        )

    sent = []

    def send(src, dst, send_sem, recv_sem, device):
        copy = remote(src, dst, send_sem, recv_sem, device)
        copy.start()
        sent.append(copy)

    for d in range(4):
        send(att_ref.at[(y + d) % NY], all_ref.at[me_global], send_sems.at[4 + d], recv_sems.at[4 + d], cross[d])
    here = remote(att_ref.at[y], all_ref.at[me_global], send_sems.at[0], recv_sems.at[0], near[0])
    local = pltpu.make_async_copy(att_ref.at[y], all_ref.at[me_global], recv_sems.at[0])

    @pl.when(stays)
    def _():
        local.start()

    @pl.when(jnp.logical_not(stays))
    def _():
        here.start()

    for d in range(1, 4):
        send(att_ref.at[(y + d) % NY], all_ref.at[me_global], send_sems.at[d], recv_sems.at[d], near[d])

    def of(source_hi, source_lo, d):
        return all_ref.at[(source_hi * 2 + source_lo) * 4 + (y + NY - d) % NY]

    for d in (0, 1, 3, 2):
        got = of(x_hi, core, d)
        if d == 0:
            @pl.when(stays)
            def _():
                local.wait()

            @pl.when(jnp.logical_not(stays))
            def _():
                here.wait_recv()
        else:
            remote(got, got, send_sems.at[d], recv_sems.at[d], near[d]).wait_recv()
        send(got, got, c_send.at[d], c_recv.at[d], twin)
    for d in (0, 1, 3, 2):
        got = of(1 - x_hi, core, d)
        remote(got, got, send_sems.at[4 + d], recv_sems.at[4 + d], cross[d]).wait_recv()
        send(got, got, c_send.at[4 + d], c_recv.at[4 + d], twin)
    for d in (0, 1, 3, 2):
        got = of(x_hi, 1 - core, d)
        remote(got, got, c_send.at[d], c_recv.at[d], twin).wait_recv()
    for d in (0, 1, 3, 2):
        got = of(1 - x_hi, 1 - core, d)
        remote(got, got, c_send.at[4 + d], c_recv.at[4 + d], twin).wait_recv()

    @pl.when(jnp.logical_not(stays))
    def _():
        here.wait_send()

    for copy in sent:
        copy.wait_send()


def give_back(attended):
    anywhere = pl.BlockSpec(memory_space=pl.ANY)
    dma = pltpu.SemaphoreType.DMA
    return pl.pallas_call(
        return_kernel,
        out_shape=jax.ShapeDtypeStruct((16, ROWS // 2, 128), BF16),
        in_specs=[anywhere],
        out_specs=anywhere,
        scratch_shapes=[dma((8,)), dma((8,)), dma((8,)), dma((8,))],
        compiler_params=pltpu.CompilerParams(collective_id=1, has_side_effects=True, vmem_limit_bytes=16 << 20),
        name="give_back",
    )(attended)


def mix_kernel(att_ref, w_ref, out_ref):
    w = w_ref[...]
    half = ROWS // 2
    for side in range(2):
        cols = slice(side * HEAD_DIM, (side + 1) * HEAD_DIM)
        a = jnp.concatenate([att_ref[g][:, cols] for g in range(16)], axis=1)
        out_ref[side * half : (side + 1) * half, :] = jnp.dot(a, w, preferred_element_type=F32).astype(BF16)


def mix(attended, w_cols):
    whole = pl.BlockSpec(memory_space=pltpu.VMEM)
    return pl.pallas_call(
        mix_kernel,
        out_shape=jax.ShapeDtypeStruct((ROWS, 256), BF16),
        in_specs=[whole, whole],
        out_specs=whole,
        compiler_params=pltpu.CompilerParams(vmem_limit_bytes=16 << 20),
        name="mix",
    )(attended, w_cols)


def body(tokens, w_query, w_key, w_value, w_out, block_mask, block_order):
    kv_all, q_all, w_all, lists = exchange(
        tokens, w_query, w_key, w_value, w_out, block_mask, block_order.reshape(1, NB)
    )
    attended = attend(lists, q_all, kv_all.reshape(32 * ROWS, 128))
    everything = give_back(attended)
    return mix(everything, w_all.reshape(1024, 256))


def solution(mesh):
    placed = (P("ctx", None), P(None, "head"), P(None, "head"), P(None, "head"), P("head", None), P(), P())
    return jax.shard_map(body, mesh=mesh, in_specs=placed, out_specs=P("ctx", "head"), check_vma=False)
```

```python
import functools

import jax
import jax.numpy as jnp
from jax import lax
from jax.experimental import pallas as pl
from jax.experimental.pallas import tpu as pltpu
from jax.sharding import PartitionSpec as P

HEAD_DIM = 64
BLOCK = 128
NB = 128
ROWS = 512
NY, NZ = 4, 4
LIST_PAD = -1e30
MESH = pl.DeviceIdType.MESH
BF16 = jnp.bfloat16
F32 = jnp.float32


def place():
    ctx = lax.axis_index("ctx")
    head = lax.axis_index("head")
    return ctx // 8, (ctx // 2) % 4, ctx % 2, head // 2, head % 2


def ctx_of(y, z, x_lo):
    return (y * NZ + z) * 2 + x_lo


def write_lists(mask, order_row, z, core, lists_ref):
    sub = lax.broadcasted_iota(jnp.int32, (NB, NB), 0)
    lane = lax.broadcasted_iota(jnp.int32, (NB, NB), 1)
    nt = (((1,), (1,)), ((), ()))

    def as_bf16(condition):
        return condition.astype(F32).astype(BF16)

    initial_of = as_bf16(order_row == sub)
    mine = ((sub // 4 * NZ + z) * 2 + core) * 4 + sub % 4
    row_pick = as_bf16(jnp.logical_and(lane == mine, sub < 16))
    rows_initial = lax.dot_general(row_pick, initial_of, nt, preferred_element_type=F32).astype(BF16)
    mask_rows = jnp.dot(rows_initial, mask.astype(F32).astype(BF16), preferred_element_type=F32).astype(BF16)
    allowed = jnp.dot(mask_rows, initial_of, preferred_element_type=F32)
    rank = jnp.dot(allowed.astype(BF16), as_bf16(sub < lane), preferred_element_type=F32)
    rank = jnp.where(allowed > 0.5, rank, -1.0)
    sub_f = sub.astype(F32)
    lane_row = lax.broadcasted_iota(jnp.int32, (8, NB), 1).astype(F32).astype(BF16)
    for i in range(16):
        hot = as_bf16(rank[i : i + 1, :] == sub_f)
        got = lax.dot_general(lane_row, hot, nt, preferred_element_type=F32)
        lists_ref[i : i + 1, :] = got[0:1, :].astype(jnp.int32)
    ones = jnp.ones((8, NB), BF16)
    count = lax.dot_general(ones, allowed.astype(BF16), nt, preferred_element_type=F32)
    steps = jnp.floor((count + 1.0) * 0.5)
    total = jnp.sum(steps, axis=1, keepdims=True)
    counts = jnp.where(lane[0:8] == 32, total, count).astype(jnp.int32)
    lists_ref[16:32, :] = jnp.zeros((16, NB), jnp.int32)
    lists_ref[17:18, :] = counts[0:1]


def query_place(i):
    b = i % 4
    return i // 4, slice(b % 2 * BLOCK, (b % 2 + 1) * BLOCK), slice(b // 2 * HEAD_DIM, (b // 2 + 1) * HEAD_DIM)


def exchange_kernel(tok_hbm, wq_hbm, wk_hbm, wv_hbm, w_ref, mask_hbm, order_hbm,
                    kv_all, ones_v, w_all, lists_ref, qz,
                    tok_ref, wq_ref, wk_ref, wv_ref, mask_ref, order_ref, kv_ref, q_ref, q_all, in_sems,
                    a_send, a_recv, q_send, q_recv, w_send, w_recv, z_send, z_recv, c_send, c_recv):
    loads = [
        pltpu.make_async_copy(src, dst, in_sems.at[n])
        for n, (src, dst) in enumerate(
            [(wk_hbm, wk_ref), (tok_hbm, tok_ref), (wv_hbm, wv_ref), (wq_hbm, wq_ref), (mask_hbm, mask_ref), (order_hbm, order_ref)]
        )
    ]
    for load in loads:
        load.start()
    y, z, x_lo, x_hi, core = place()
    me_ctx = ctx_of(y, z, x_lo)
    me_head = x_hi * 2 + core
    swap_head = x_hi * 2 + x_lo
    stays = x_lo == core
    up = (ctx_of(y, (z + 1) % NZ, x_lo), me_head)
    down = (ctx_of(y, (z + 3) % NZ, x_lo), me_head)
    twin = (me_ctx, x_hi * 2 + 1 - core)
    head_peers = [(me_ctx, (me_head + k) % 4) for k in range(1, 4)]
    a_to = [(ctx_of((y + d) % NY, z, core), swap_head) for d in range(4)]

    barrier = pltpu.get_barrier_semaphore()
    for peer in [up, down, *head_peers, *a_to[1:]]:
        pl.semaphore_signal(barrier, inc=1, device_id=peer, device_id_type=MESH)

    @pl.when(jnp.logical_not(stays))
    def _():
        pl.semaphore_signal(barrier, inc=1, device_id=a_to[0], device_id_type=MESH)

    half = ROWS // 2
    columns = [slice(j * HEAD_DIM, (j + 1) * HEAD_DIM) for j in range(4)]
    loads[0].wait()
    loads[1].wait()
    tok = tok_ref[...]
    keys = jnp.dot(tok, wk_ref[...], preferred_element_type=F32).astype(BF16)
    loads[2].wait()
    vals = jnp.dot(tok, wv_ref[...], preferred_element_type=F32).astype(BF16)
    for j in range(4):
        kv_ref[j] = jnp.concatenate([keys[:, columns[j]], vals[:, columns[j]]], axis=1)

    pl.semaphore_wait(barrier, 8 + (x_lo + core) % 2)

    def remote(src, dst, send_sem, recv_sem, device):
        return pltpu.make_async_remote_copy(
            src_ref=src, dst_ref=dst, send_sem=send_sem, recv_sem=recv_sem, device_id=device, device_id_type=MESH
        )

    sent = []

    def send(src, dst, send_sem, recv_sem, device):
        copy = remote(src, dst, send_sem, recv_sem, device)
        copy.start()
        sent.append(copy)

    def arrived(dst, send_sem, recv_sem, device):
        remote(dst, dst, send_sem, recv_sem, device).wait_recv()

    own = y % NY
    kv_here = remote(kv_ref.at[own], kv_all.at[me_ctx], a_send.at[0], a_recv.at[0], a_to[0])
    q_here = remote(q_ref.at[own], q_all.at[y], q_send.at[0], q_recv.at[0], a_to[0])
    kv_local = pltpu.make_async_copy(kv_ref.at[own], kv_all.at[me_ctx], a_recv.at[0])
    q_local = pltpu.make_async_copy(q_ref.at[own], q_all.at[y], q_recv.at[0])

    @pl.when(stays)
    def _():
        kv_local.start()

    @pl.when(jnp.logical_not(stays))
    def _():
        kv_here.start()

    def send_kv(d):
        send(kv_ref.at[(y + d) % NY], kv_all.at[me_ctx], a_send.at[d], a_recv.at[d], a_to[d])

    def send_q(d):
        send(q_ref.at[(y + d) % NY], q_all.at[y], q_send.at[d], q_recv.at[d], a_to[d])

    def chunk(d, dz):
        return kv_all.at[ctx_of((y + NY - d) % NY, (z + NZ + dz) % NZ, core)]

    def pass_on(d):
        send(chunk(d, 0), chunk(d, 0), z_send.at[d], z_recv.at[d], up)
        send(chunk(d, 0), chunk(d, 0), z_send.at[4 + d], z_recv.at[4 + d], down)
        send(chunk(d, 0), chunk(d, 0), c_send.at[d], c_recv.at[d], twin)

    def from_near(d):
        below, above = chunk(d, -1), chunk(d, 1)
        arrived(below, z_send.at[d], z_recv.at[d], up)
        if d in (0, 1):
            send(below, below, z_send.at[8 + d], z_recv.at[8 + d], up)
        send(below, below, c_send.at[4 + d], c_recv.at[4 + d], twin)
        arrived(above, z_send.at[4 + d], z_recv.at[4 + d], down)
        if d in (2, 3):
            send(above, above, z_send.at[8 + d], z_recv.at[8 + d], down)
        send(above, above, c_send.at[8 + d], c_recv.at[8 + d], twin)

    order = (1, 3, 2)
    send_kv(1)
    send_kv(3)
    send_kv(2)

    @pl.when(stays)
    def _():
        kv_local.wait()

    @pl.when(jnp.logical_not(stays))
    def _():
        kv_here.wait_recv()

    pass_on(0)
    loads[3].wait()
    query = jnp.dot(tok, wq_ref[...], preferred_element_type=F32).astype(BF16)
    for j in range(4):
        q_ref[j] = jnp.concatenate([query[:half, columns[j]], query[half:, columns[j]]], axis=1)

    @pl.when(stays)
    def _():
        q_local.start()

    @pl.when(jnp.logical_not(stays))
    def _():
        q_here.start()

    for d in order:
        send_q(d)
    arrived(chunk(1, 0), a_send.at[1], a_recv.at[1], a_to[1])
    pass_on(1)
    arrived(chunk(3, 0), a_send.at[3], a_recv.at[3], a_to[3])
    pass_on(3)
    arrived(chunk(2, 0), a_send.at[2], a_recv.at[2], a_to[2])
    pass_on(2)
    from_near(0)
    for k in range(1, 4):
        to = (me_head + k) % 4
        send(w_ref.at[:, pl.ds(pl.multiple_of(to * 256, 256), 256)], w_all.at[me_head], w_send.at[k - 1], w_recv.at[k - 1],
             head_peers[k - 1])
    w_local = pltpu.make_async_copy(
        w_ref.at[:, pl.ds(pl.multiple_of(me_head * 256, 256), 256)], w_all.at[me_head], w_recv.at[3]
    )
    w_local.start()
    from_near(1)
    loads[4].wait()
    loads[5].wait()
    write_lists(mask_ref[...], order_ref[...], z, core, lists_ref)

    def twin_arrived(d, dz, place_of):
        got = kv_all.at[ctx_of((y + NY - d) % NY, (z + NZ + dz) % NZ, 1 - core)]
        arrived(got, c_send.at[place_of + d], c_recv.at[place_of + d], twin)

    left = lax.broadcasted_iota(jnp.int32, (ROWS, 128), 1) < HEAD_DIM

    def lay_out(d, dz, sides=(0, 1)):
        for side in sides:
            ctx = ctx_of((y + NY - d) % NY, (z + NZ + dz) % NZ, side)
            rows = pl.ds(pl.multiple_of(ctx * ROWS, ROWS), ROWS)
            got = kv_all[ctx]
            ones_v[rows, :] = jnp.where(left, jnp.ones_like(got), got)

    @pl.when(stays)
    def _():
        q_local.wait()

    @pl.when(jnp.logical_not(stays))
    def _():
        q_here.wait_recv()

    for d in order:
        arrived(q_all.at[(y + NY - d) % NY], q_send.at[d], q_recv.at[d], a_to[d])
    narrow = lax.broadcasted_iota(jnp.int32, (BLOCK, 128), 1) < HEAD_DIM
    for i in range(16):
        step, rows, cols = query_place(i)
        q = q_all[step, rows, :]
        if cols.start:
            q = jnp.concatenate([q[:, HEAD_DIM:], q[:, :HEAD_DIM]], axis=1)
        qz[i] = jnp.where(narrow, q, jnp.zeros_like(q))
    qz[16] = jnp.zeros((BLOCK, 128), BF16)
    for d in (0, 1, 3, 2):
        twin_arrived(d, 0, 0)
        lay_out(d, 0)
    from_near(3)
    from_near(2)
    for d in (0, 1, 3, 2):
        twin_arrived(d, -1, 4)
        twin_arrived(d, 1, 8)
        lay_out(d, -1)
        lay_out(d, 1)
    for d in (0, 1, 3, 2):
        far = chunk(d, 2)
        arrived(far, z_send.at[8 + d], z_recv.at[8 + d], up)
        send(far, far, c_send.at[12 + d], c_recv.at[12 + d], twin)
        lay_out(d, 2, (core,))
    for d in (0, 1, 3, 2):
        twin_arrived(d, 2, 12)
        lay_out(d, 2, (1 - core,))

    @pl.when(jnp.logical_not(stays))
    def _():
        kv_here.wait_send()
        q_here.wait_send()

    for k in range(1, 4):
        arrived(w_all.at[(me_head + 4 - k) % 4], w_send.at[k - 1], w_recv.at[k - 1], head_peers[k - 1])
    w_local.wait()
    for copy in sent:
        copy.wait_send()


def exchange(tokens, w_query, w_key, w_value, w_out, block_mask, order_row):
    in_hbm = pl.BlockSpec(memory_space=pltpu.HBM)
    operands = [tokens, w_query, w_key, w_value, w_out, block_mask, order_row]
    operands = [pltpu.with_memory_space_constraint(a, pltpu.HBM) for a in operands]
    anywhere = pl.BlockSpec(memory_space=pl.ANY)
    dma = pltpu.SemaphoreType.DMA
    vmem = pltpu.VMEM
    in_vmem = pl.BlockSpec(memory_space=vmem)
    return pl.pallas_call(
        exchange_kernel,
        out_shape=(
            jax.ShapeDtypeStruct((32, ROWS, 128), BF16),
            jax.ShapeDtypeStruct((32 * ROWS, 128), BF16),
            jax.ShapeDtypeStruct((4, 256, 256), BF16),
            jax.ShapeDtypeStruct((32, NB), jnp.int32),
            jax.ShapeDtypeStruct((17, BLOCK, 128), BF16),
        ),
        in_specs=[in_hbm] * 7,
        out_specs=(in_vmem, in_vmem, anywhere, in_vmem, in_vmem),
        scratch_shapes=[
            vmem((ROWS, 1024), BF16), vmem((1024, 256), BF16), vmem((1024, 256), BF16), vmem((1024, 256), BF16),
            vmem((NB, NB), jnp.int32), vmem((1, NB), jnp.int32), vmem((4, ROWS, 128), BF16), vmem((4, ROWS // 2, 128), BF16),
            vmem((4, ROWS // 2, 128), BF16), dma((6,)),
            dma((4,)), dma((4,)), dma((4,)), dma((4,)), dma((4,)), dma((4,)),
            dma((12,)), dma((12,)), dma((16,)), dma((16,)),
        ],
        compiler_params=pltpu.CompilerParams(collective_id=0, has_side_effects=True, vmem_limit_bytes=24 << 20),
        name="exchange",
    )(*operands)


UNROLL = 8
EXP2_SCALE = (HEAD_DIM ** -0.5) * 1.4426950408889634
SMALLEST, LARGEST = 1e-20, 1e30
NT = (((1,), (1,)), ((), ()))


def attend_kernel(lists, kv_ref, ones_v, qz, out_ref, acc, sbuf, scores):
    zero = jnp.zeros((BLOCK, 128), F32)
    for i in range(17):
        acc[i] = zero
    second = lax.broadcasted_iota(jnp.int32, (1, 2 * BLOCK), 1) >= BLOCK

    def rows_at(i, k):
        return pl.ds(pl.multiple_of(lists[i, jnp.minimum(k, NB - 1)] * BLOCK, BLOCK), BLOCK)

    def advance(i, k):
        done = k + 2 >= lists[17, i]
        return jnp.minimum(jnp.where(done, i + 1, i), 16), jnp.where(done, 0, k + 2)

    def score(slot, i, k):
        for u in range(UNROLL):
            keys = jnp.concatenate([kv_ref[rows_at(i, k), :], kv_ref[rows_at(i, k + 1), :]], axis=0)
            sbuf[slot, u] = lax.dot_general(qz[i], keys, NT, preferred_element_type=F32)
            i, k = advance(i, k)
        return i, k

    def weigh(slot, i, k):
        for u in range(UNROLL):
            bias = jnp.where(k + 1 < lists[17, i], 0.0, LIST_PAD).astype(F32)
            vals = jnp.concatenate([ones_v[rows_at(i, k), :], ones_v[rows_at(i, k + 1), :]], axis=0)
            p = jnp.exp2(sbuf[slot, u] * EXP2_SCALE + jnp.where(second, bias, 0.0)).astype(BF16)
            acc[i] += jnp.dot(p, vals, preferred_element_type=F32)
            i, k = advance(i, k)

    start = jnp.int32(0)
    i1, k1 = score(0, start, start)

    def step(_, carry):
        i, k, i1, k1 = carry
        i2, k2 = score(1, i1, k1)
        weigh(0, i, k)
        i3, k3 = score(0, i2, k2)
        weigh(1, i1, k1)
        return i2, k2, i3, k3

    lax.fori_loop(0, (lists[17, 32] + 2 * UNROLL - 1) // (2 * UNROLL), step, (start, start, i1, k1))

    fine = jnp.full((BLOCK, HEAD_DIM), 1.0, F32)
    for i in range(16):
        y, rows, cols = query_place(i)
        denom = acc[i][:, :HEAD_DIM]
        within = jnp.logical_and(denom >= SMALLEST, denom <= LARGEST)
        fine = jnp.where(within, fine, 0.0)
        out_ref[y, rows, cols] = (acc[i][:, HEAD_DIM:] / denom).astype(BF16)

    @pl.when(jnp.min(fine) < 0.5)
    def _():
        for i in range(16):
            y, rows, cols = query_place(i)
            n = lists[17, i]

            def first(k, top):
                s = lax.dot_general(qz[i], kv_ref[rows_at(i, k), :], NT, preferred_element_type=F32)
                scores[k] = s
                return jnp.maximum(top, s)

            top = lax.fori_loop(0, n, first, jnp.full((BLOCK, BLOCK), -3e38, F32))
            top = jnp.max(top, axis=1, keepdims=True)

            def then(k, carry):
                total, weighted = carry
                p = jnp.exp2((scores[k] - top) * EXP2_SCALE)
                return total + p, weighted + jnp.dot(
                    p.astype(BF16), kv_ref[rows_at(i, k), :], preferred_element_type=F32
                )

            total, weighted = lax.fori_loop(0, n, then, (zero, zero))
            denom = jnp.sum(total, axis=1, keepdims=True)
            out_ref[y, rows, cols] = (weighted[:, HEAD_DIM:] / denom).astype(BF16)


def attend(lists, kv, ones_v, qz):
    whole = pl.BlockSpec(memory_space=pltpu.VMEM)
    vmem = pltpu.VMEM
    return pl.pallas_call(
        attend_kernel,
        out_shape=jax.ShapeDtypeStruct((4, ROWS // 2, 128), BF16),
        grid_spec=pltpu.PrefetchScalarGridSpec(
            num_scalar_prefetch=1,
            grid=(),
            in_specs=[whole] * 3,
            out_specs=whole,
            scratch_shapes=[
                vmem((17, BLOCK, 128), F32),
                vmem((2, UNROLL, BLOCK, 2 * BLOCK), F32),
                vmem((NB, BLOCK, BLOCK), F32),
            ],
        ),
        compiler_params=pltpu.CompilerParams(vmem_limit_bytes=24 << 20),
        name="attend",
    )(lists, kv, ones_v, qz)


def return_kernel(att_ref, all_ref, send_sems, recv_sems, c_send, c_recv):
    y, z, x_lo, x_hi, core = place()
    me_ctx = ctx_of(y, z, x_lo)
    stays = x_lo == core
    twin = (me_ctx, x_hi * 2 + 1 - core)
    me_global = (x_hi * 2 + x_lo) * 4 + y
    near = [(ctx_of((y + d) % NY, z, core), x_hi * 2 + x_lo) for d in range(4)]
    cross = [(ctx_of((y + d) % NY, z, core), (1 - x_hi) * 2 + x_lo) for d in range(4)]

    barrier = pltpu.get_barrier_semaphore()
    for peer in [twin, *cross, *near[1:]]:
        pl.semaphore_signal(barrier, inc=1, device_id=peer, device_id_type=MESH)

    @pl.when(jnp.logical_not(stays))
    def _():
        pl.semaphore_signal(barrier, inc=1, device_id=near[0], device_id_type=MESH)

    pl.semaphore_wait(barrier, 8 + (x_lo + core) % 2)

    def remote(src, dst, send_sem, recv_sem, device):
        return pltpu.make_async_remote_copy(
            src_ref=src, dst_ref=dst, send_sem=send_sem, recv_sem=recv_sem, device_id=device, device_id_type=MESH
        )

    sent = []

    def send(src, dst, send_sem, recv_sem, device):
        copy = remote(src, dst, send_sem, recv_sem, device)
        copy.start()
        sent.append(copy)

    for d in range(4):
        send(att_ref.at[(y + d) % NY], all_ref.at[me_global], send_sems.at[4 + d], recv_sems.at[4 + d], cross[d])
    here = remote(att_ref.at[y], all_ref.at[me_global], send_sems.at[0], recv_sems.at[0], near[0])
    local = pltpu.make_async_copy(att_ref.at[y], all_ref.at[me_global], recv_sems.at[0])

    @pl.when(stays)
    def _():
        local.start()

    @pl.when(jnp.logical_not(stays))
    def _():
        here.start()

    for d in range(1, 4):
        send(att_ref.at[(y + d) % NY], all_ref.at[me_global], send_sems.at[d], recv_sems.at[d], near[d])

    def of(source_hi, source_lo, d):
        return all_ref.at[(source_hi * 2 + source_lo) * 4 + (y + NY - d) % NY]

    for d in (0, 1, 3, 2):
        got = of(x_hi, core, d)
        if d == 0:
            @pl.when(stays)
            def _():
                local.wait()

            @pl.when(jnp.logical_not(stays))
            def _():
                here.wait_recv()
        else:
            remote(got, got, send_sems.at[d], recv_sems.at[d], near[d]).wait_recv()
        send(got, got, c_send.at[d], c_recv.at[d], twin)
    for d in (0, 1, 3, 2):
        got = of(1 - x_hi, core, d)
        remote(got, got, send_sems.at[4 + d], recv_sems.at[4 + d], cross[d]).wait_recv()
        send(got, got, c_send.at[4 + d], c_recv.at[4 + d], twin)
    for d in (0, 1, 3, 2):
        got = of(x_hi, 1 - core, d)
        remote(got, got, c_send.at[d], c_recv.at[d], twin).wait_recv()
    for d in (0, 1, 3, 2):
        got = of(1 - x_hi, 1 - core, d)
        remote(got, got, c_send.at[4 + d], c_recv.at[4 + d], twin).wait_recv()

    @pl.when(jnp.logical_not(stays))
    def _():
        here.wait_send()

    for copy in sent:
        copy.wait_send()


def give_back(attended):
    anywhere = pl.BlockSpec(memory_space=pl.ANY)
    dma = pltpu.SemaphoreType.DMA
    return pl.pallas_call(
        return_kernel,
        out_shape=jax.ShapeDtypeStruct((16, ROWS // 2, 128), BF16),
        in_specs=[anywhere],
        out_specs=anywhere,
        scratch_shapes=[dma((8,)), dma((8,)), dma((8,)), dma((8,))],
        compiler_params=pltpu.CompilerParams(collective_id=1, has_side_effects=True, vmem_limit_bytes=16 << 20),
        name="give_back",
    )(attended)


def mix_kernel(att_ref, w_ref, out_ref):
    w = w_ref[...]
    half = ROWS // 2
    for side in range(2):
        cols = slice(side * HEAD_DIM, (side + 1) * HEAD_DIM)
        a = jnp.concatenate([att_ref[g][:, cols] for g in range(16)], axis=1)
        out_ref[side * half : (side + 1) * half, :] = jnp.dot(a, w, preferred_element_type=F32).astype(BF16)


def mix(attended, w_cols):
    whole = pl.BlockSpec(memory_space=pltpu.VMEM)
    return pl.pallas_call(
        mix_kernel,
        out_shape=jax.ShapeDtypeStruct((ROWS, 256), BF16),
        in_specs=[whole, whole],
        out_specs=whole,
        compiler_params=pltpu.CompilerParams(vmem_limit_bytes=16 << 20),
        name="mix",
    )(attended, w_cols)


def body(tokens, w_query, w_key, w_value, w_out, block_mask, block_order):
    kv, ones_v, w_all, lists, qz = exchange(
        tokens, w_query, w_key, w_value, w_out, block_mask, block_order.reshape(1, NB)
    )
    attended = attend(lists, kv.reshape(32 * ROWS, 128), ones_v, qz)
    everything = give_back(attended)
    return mix(everything, w_all.reshape(1024, 256))


def solution(mesh):
    placed = (P("ctx", None), P(None, "head"), P(None, "head"), P(None, "head"), P("head", None), P(), P())
    return jax.shard_map(body, mesh=mesh, in_specs=placed, out_specs=P("ctx", "head"), check_vma=False)
```

```python
import functools

import jax
import jax.numpy as jnp
from jax import lax
from jax.experimental import pallas as pl
from jax.experimental.pallas import tpu as pltpu
from jax.sharding import PartitionSpec as P

HEAD_DIM = 64
BLOCK = 128
NB = 128
ROWS = 512
NY, NZ = 4, 4
LIST_PAD = -1e30
MESH = pl.DeviceIdType.MESH
BF16 = jnp.bfloat16
F32 = jnp.float32


def place():
    ctx = lax.axis_index("ctx")
    head = lax.axis_index("head")
    return ctx // 8, (ctx // 2) % 4, ctx % 2, head // 2, head % 2


def ctx_of(y, z, x_lo):
    return (y * NZ + z) * 2 + x_lo


def write_lists(mask, order_row, z, core, lists_ref):
    sub = lax.broadcasted_iota(jnp.int32, (NB, NB), 0)
    lane = lax.broadcasted_iota(jnp.int32, (NB, NB), 1)
    nt = (((1,), (1,)), ((), ()))

    def as_bf16(condition):
        return condition.astype(F32).astype(BF16)

    initial_of = as_bf16(order_row == sub)
    mine = ((sub // 4 * NZ + z) * 2 + core) * 4 + sub % 4
    row_pick = as_bf16(jnp.logical_and(lane == mine, sub < 16))
    rows_initial = lax.dot_general(row_pick, initial_of, nt, preferred_element_type=F32).astype(BF16)
    mask_rows = jnp.dot(rows_initial, mask.astype(F32).astype(BF16), preferred_element_type=F32).astype(BF16)
    allowed = jnp.dot(mask_rows, initial_of, preferred_element_type=F32)
    rank = jnp.dot(allowed.astype(BF16), as_bf16(sub < lane), preferred_element_type=F32)
    rank = jnp.where(allowed > 0.5, rank, -1.0)
    sub_f = sub.astype(F32)
    lane_row = lax.broadcasted_iota(jnp.int32, (8, NB), 1).astype(F32).astype(BF16)
    for i in range(16):
        hot = as_bf16(rank[i : i + 1, :] == sub_f)
        got = lax.dot_general(lane_row, hot, nt, preferred_element_type=F32)
        lists_ref[i : i + 1, :] = got[0:1, :].astype(jnp.int32)
    ones = jnp.ones((8, NB), BF16)
    count = lax.dot_general(ones, allowed.astype(BF16), nt, preferred_element_type=F32)
    steps = jnp.floor((count + 1.0) * 0.5)
    total = jnp.sum(steps, axis=1, keepdims=True)
    counts = jnp.where(lane[0:8] == 32, total, count).astype(jnp.int32)
    lists_ref[16:32, :] = jnp.zeros((16, NB), jnp.int32)
    lists_ref[17:18, :] = counts[0:1]


def query_place(i):
    b = i % 4
    return i // 4, slice(b % 2 * BLOCK, (b % 2 + 1) * BLOCK), slice(b // 2 * HEAD_DIM, (b // 2 + 1) * HEAD_DIM)


def exchange_kernel(tok_hbm, wq_hbm, wk_hbm, wv_hbm, w_ref, mask_hbm, order_hbm,
                    kv_all, ones_v, w_all, lists_ref, qz,
                    tok_ref, wq_ref, wk_ref, wv_ref, mask_ref, order_ref, kv_ref, q_ref, q_all, in_sems,
                    a_send, a_recv, q_send, q_recv, w_send, w_recv, z_send, z_recv, c_send, c_recv):
    loads = [
        pltpu.make_async_copy(src, dst, in_sems.at[n])
        for n, (src, dst) in enumerate(
            [(wk_hbm, wk_ref), (tok_hbm, tok_ref), (wv_hbm, wv_ref), (wq_hbm, wq_ref), (mask_hbm, mask_ref), (order_hbm, order_ref)]
        )
    ]
    for load in loads:
        load.start()
    y, z, x_lo, x_hi, core = place()
    me_ctx = ctx_of(y, z, x_lo)
    me_head = x_hi * 2 + core
    swap_head = x_hi * 2 + x_lo
    stays = x_lo == core
    up = (ctx_of(y, (z + 1) % NZ, x_lo), me_head)
    down = (ctx_of(y, (z + 3) % NZ, x_lo), me_head)
    twin = (me_ctx, x_hi * 2 + 1 - core)
    head_peers = [(me_ctx, (me_head + k) % 4) for k in range(1, 4)]
    a_to = [(ctx_of((y + d) % NY, z, core), swap_head) for d in range(4)]

    barrier = pltpu.get_barrier_semaphore()
    for peer in [up, down, *head_peers, *a_to[1:]]:
        pl.semaphore_signal(barrier, inc=1, device_id=peer, device_id_type=MESH)

    @pl.when(jnp.logical_not(stays))
    def _():
        pl.semaphore_signal(barrier, inc=1, device_id=a_to[0], device_id_type=MESH)

    half = ROWS // 2
    columns = [slice(j * HEAD_DIM, (j + 1) * HEAD_DIM) for j in range(4)]
    loads[0].wait()
    loads[1].wait()
    tok = tok_ref[...]
    keys = jnp.dot(tok, wk_ref[...], preferred_element_type=F32).astype(BF16)
    loads[2].wait()
    vals = jnp.dot(tok, wv_ref[...], preferred_element_type=F32).astype(BF16)
    for j in range(4):
        kv_ref[j] = jnp.concatenate([keys[:, columns[j]], vals[:, columns[j]]], axis=1)

    pl.semaphore_wait(barrier, 8 + (x_lo + core) % 2)

    def remote(src, dst, send_sem, recv_sem, device):
        return pltpu.make_async_remote_copy(
            src_ref=src, dst_ref=dst, send_sem=send_sem, recv_sem=recv_sem, device_id=device, device_id_type=MESH
        )

    sent = []

    def send(src, dst, send_sem, recv_sem, device):
        copy = remote(src, dst, send_sem, recv_sem, device)
        copy.start()
        sent.append(copy)

    def arrived(dst, send_sem, recv_sem, device):
        remote(dst, dst, send_sem, recv_sem, device).wait_recv()

    own = y % NY
    kv_here = remote(kv_ref.at[own], kv_all.at[me_ctx], a_send.at[0], a_recv.at[0], a_to[0])
    q_here = remote(q_ref.at[own], q_all.at[y], q_send.at[0], q_recv.at[0], a_to[0])
    kv_local = pltpu.make_async_copy(kv_ref.at[own], kv_all.at[me_ctx], a_recv.at[0])
    q_local = pltpu.make_async_copy(q_ref.at[own], q_all.at[y], q_recv.at[0])

    @pl.when(stays)
    def _():
        kv_local.start()

    @pl.when(jnp.logical_not(stays))
    def _():
        kv_here.start()

    def send_kv(d):
        send(kv_ref.at[(y + d) % NY], kv_all.at[me_ctx], a_send.at[d], a_recv.at[d], a_to[d])

    def send_q(d):
        send(q_ref.at[(y + d) % NY], q_all.at[y], q_send.at[d], q_recv.at[d], a_to[d])

    def chunk(d, dz):
        return kv_all.at[ctx_of((y + NY - d) % NY, (z + NZ + dz) % NZ, core)]

    def pass_on(d):
        send(chunk(d, 0), chunk(d, 0), z_send.at[d], z_recv.at[d], up)
        send(chunk(d, 0), chunk(d, 0), z_send.at[4 + d], z_recv.at[4 + d], down)
        send(chunk(d, 0), chunk(d, 0), c_send.at[d], c_recv.at[d], twin)

    def from_near(d):
        below, above = chunk(d, -1), chunk(d, 1)
        arrived(below, z_send.at[d], z_recv.at[d], up)
        if d in (0, 1):
            send(below, below, z_send.at[8 + d], z_recv.at[8 + d], up)
        send(below, below, c_send.at[4 + d], c_recv.at[4 + d], twin)
        arrived(above, z_send.at[4 + d], z_recv.at[4 + d], down)
        if d in (2, 3):
            send(above, above, z_send.at[8 + d], z_recv.at[8 + d], down)
        send(above, above, c_send.at[8 + d], c_recv.at[8 + d], twin)

    order = (1, 3, 2)
    send_kv(1)
    send_kv(3)
    send_kv(2)

    @pl.when(stays)
    def _():
        kv_local.wait()

    @pl.when(jnp.logical_not(stays))
    def _():
        kv_here.wait_recv()

    pass_on(0)
    loads[3].wait()
    query = jnp.dot(tok, wq_ref[...], preferred_element_type=F32).astype(BF16)
    for j in range(4):
        q_ref[j] = jnp.concatenate([query[:half, columns[j]], query[half:, columns[j]]], axis=1)

    @pl.when(stays)
    def _():
        q_local.start()

    @pl.when(jnp.logical_not(stays))
    def _():
        q_here.start()

    for d in order:
        send_q(d)
    arrived(chunk(1, 0), a_send.at[1], a_recv.at[1], a_to[1])
    pass_on(1)
    arrived(chunk(3, 0), a_send.at[3], a_recv.at[3], a_to[3])
    pass_on(3)
    arrived(chunk(2, 0), a_send.at[2], a_recv.at[2], a_to[2])
    pass_on(2)
    from_near(0)
    for k in range(1, 4):
        to = (me_head + k) % 4
        send(w_ref.at[:, pl.ds(pl.multiple_of(to * 256, 256), 256)], w_all.at[me_head], w_send.at[k - 1], w_recv.at[k - 1],
             head_peers[k - 1])
    w_local = pltpu.make_async_copy(
        w_ref.at[:, pl.ds(pl.multiple_of(me_head * 256, 256), 256)], w_all.at[me_head], w_recv.at[3]
    )
    w_local.start()
    from_near(1)
    loads[4].wait()
    loads[5].wait()
    write_lists(mask_ref[...], order_ref[...], z, core, lists_ref)

    def twin_arrived(d, dz, place_of):
        got = kv_all.at[ctx_of((y + NY - d) % NY, (z + NZ + dz) % NZ, 1 - core)]
        arrived(got, c_send.at[place_of + d], c_recv.at[place_of + d], twin)

    left = lax.broadcasted_iota(jnp.int32, (ROWS, 128), 1) < HEAD_DIM

    def lay_out(d, dz, sides=(0, 1)):
        for side in sides:
            ctx = ctx_of((y + NY - d) % NY, (z + NZ + dz) % NZ, side)
            rows = pl.ds(pl.multiple_of(ctx * ROWS, ROWS), ROWS)
            got = kv_all[ctx]
            ones_v[rows, :] = jnp.where(left, jnp.ones_like(got), got)

    @pl.when(stays)
    def _():
        q_local.wait()

    @pl.when(jnp.logical_not(stays))
    def _():
        q_here.wait_recv()

    for d in order:
        arrived(q_all.at[(y + NY - d) % NY], q_send.at[d], q_recv.at[d], a_to[d])
    narrow = lax.broadcasted_iota(jnp.int32, (BLOCK, 128), 1) < HEAD_DIM
    for i in range(16):
        step, rows, cols = query_place(i)
        q = q_all[step, rows, :]
        if cols.start:
            q = jnp.concatenate([q[:, HEAD_DIM:], q[:, :HEAD_DIM]], axis=1)
        qz[i] = jnp.where(narrow, q, jnp.zeros_like(q))
    qz[16] = jnp.zeros((BLOCK, 128), BF16)
    for d in (0, 1, 3, 2):
        twin_arrived(d, 0, 0)
        lay_out(d, 0)
    from_near(3)
    from_near(2)
    for d in (0, 1, 3, 2):
        twin_arrived(d, -1, 4)
        twin_arrived(d, 1, 8)
        lay_out(d, -1)
        lay_out(d, 1)
    for d in (0, 1, 3, 2):
        far = chunk(d, 2)
        arrived(far, z_send.at[8 + d], z_recv.at[8 + d], up)
        send(far, far, c_send.at[12 + d], c_recv.at[12 + d], twin)
        lay_out(d, 2, (core,))
    for d in (0, 1, 3, 2):
        twin_arrived(d, 2, 12)
        lay_out(d, 2, (1 - core,))

    @pl.when(jnp.logical_not(stays))
    def _():
        kv_here.wait_send()
        q_here.wait_send()

    for k in range(1, 4):
        arrived(w_all.at[(me_head + 4 - k) % 4], w_send.at[k - 1], w_recv.at[k - 1], head_peers[k - 1])
    w_local.wait()
    for copy in sent:
        copy.wait_send()


def exchange(tokens, w_query, w_key, w_value, w_out, block_mask, order_row):
    in_hbm = pl.BlockSpec(memory_space=pltpu.HBM)
    operands = [tokens, w_query, w_key, w_value, w_out, block_mask, order_row]
    operands = [pltpu.with_memory_space_constraint(a, pltpu.HBM) for a in operands]
    anywhere = pl.BlockSpec(memory_space=pl.ANY)
    dma = pltpu.SemaphoreType.DMA
    vmem = pltpu.VMEM
    in_vmem = pl.BlockSpec(memory_space=vmem)
    return pl.pallas_call(
        exchange_kernel,
        out_shape=(
            jax.ShapeDtypeStruct((32, ROWS, 128), BF16),
            jax.ShapeDtypeStruct((32 * ROWS, 128), BF16),
            jax.ShapeDtypeStruct((4, 256, 256), BF16),
            jax.ShapeDtypeStruct((32, NB), jnp.int32),
            jax.ShapeDtypeStruct((17, BLOCK, 128), BF16),
        ),
        in_specs=[in_hbm] * 7,
        out_specs=(in_vmem, in_vmem, anywhere, in_vmem, in_vmem),
        scratch_shapes=[
            vmem((ROWS, 1024), BF16), vmem((1024, 256), BF16), vmem((1024, 256), BF16), vmem((1024, 256), BF16),
            vmem((NB, NB), jnp.int32), vmem((1, NB), jnp.int32), vmem((4, ROWS, 128), BF16), vmem((4, ROWS // 2, 128), BF16),
            vmem((4, ROWS // 2, 128), BF16), dma((6,)),
            dma((4,)), dma((4,)), dma((4,)), dma((4,)), dma((4,)), dma((4,)),
            dma((12,)), dma((12,)), dma((16,)), dma((16,)),
        ],
        compiler_params=pltpu.CompilerParams(collective_id=0, has_side_effects=True, vmem_limit_bytes=24 << 20),
        name="exchange",
    )(*operands)


UNROLL = 7
EXP2_SCALE = (HEAD_DIM ** -0.5) * 1.4426950408889634
SMALLEST, LARGEST = 1e-20, 1e30
NT = (((1,), (1,)), ((), ()))


def attend_kernel(lists, kv_ref, ones_v, qz, out_ref, acc, sbuf, scores):
    zero = jnp.zeros((BLOCK, 128), F32)
    for i in range(17):
        acc[i] = zero
    second = lax.broadcasted_iota(jnp.int32, (1, 2 * BLOCK), 1) >= BLOCK

    def rows_at(i, k):
        return pl.ds(pl.multiple_of(lists[i, jnp.minimum(k, NB - 1)] * BLOCK, BLOCK), BLOCK)

    def advance(i, k):
        done = k + 2 >= lists[17, i]
        return jnp.minimum(jnp.where(done, i + 1, i), 16), jnp.where(done, 0, k + 2)

    def score(slot, i, k):
        for u in range(UNROLL):
            keys = jnp.concatenate([kv_ref[rows_at(i, k), :], kv_ref[rows_at(i, k + 1), :]], axis=0)
            sbuf[slot, u] = lax.dot_general(qz[i], keys, NT, preferred_element_type=F32)
            i, k = advance(i, k)
        return i, k

    def weigh(slot, i, k):
        for u in range(UNROLL):
            bias = jnp.where(k + 1 < lists[17, i], 0.0, LIST_PAD).astype(F32)
            vals = jnp.concatenate([ones_v[rows_at(i, k), :], ones_v[rows_at(i, k + 1), :]], axis=0)
            p = jnp.exp2(sbuf[slot, u] * EXP2_SCALE + jnp.where(second, bias, 0.0)).astype(BF16)
            acc[i] += jnp.dot(p, vals, preferred_element_type=F32)
            i, k = advance(i, k)

    start = jnp.int32(0)
    i1, k1 = score(0, start, start)

    def step(_, carry):
        i, k, i1, k1 = carry
        i2, k2 = score(1, i1, k1)
        weigh(0, i, k)
        i3, k3 = score(0, i2, k2)
        weigh(1, i1, k1)
        return i2, k2, i3, k3

    lax.fori_loop(0, (lists[17, 32] + 2 * UNROLL - 1) // (2 * UNROLL), step, (start, start, i1, k1))

    fine = jnp.full((BLOCK, HEAD_DIM), 1.0, F32)
    for i in range(16):
        y, rows, cols = query_place(i)
        denom = acc[i][:, :HEAD_DIM]
        within = jnp.logical_and(denom >= SMALLEST, denom <= LARGEST)
        fine = jnp.where(within, fine, 0.0)
        out_ref[y, rows, cols] = (acc[i][:, HEAD_DIM:] / denom).astype(BF16)

    @pl.when(jnp.min(fine) < 0.5)
    def _():
        for i in range(16):
            y, rows, cols = query_place(i)
            n = lists[17, i]

            def first(k, top):
                s = lax.dot_general(qz[i], kv_ref[rows_at(i, k), :], NT, preferred_element_type=F32)
                scores[k] = s
                return jnp.maximum(top, s)

            top = lax.fori_loop(0, n, first, jnp.full((BLOCK, BLOCK), -3e38, F32))
            top = jnp.max(top, axis=1, keepdims=True)

            def then(k, carry):
                total, weighted = carry
                p = jnp.exp2((scores[k] - top) * EXP2_SCALE)
                return total + p, weighted + jnp.dot(
                    p.astype(BF16), kv_ref[rows_at(i, k), :], preferred_element_type=F32
                )

            total, weighted = lax.fori_loop(0, n, then, (zero, zero))
            denom = jnp.sum(total, axis=1, keepdims=True)
            out_ref[y, rows, cols] = (weighted[:, HEAD_DIM:] / denom).astype(BF16)


def attend(lists, kv, ones_v, qz):
    whole = pl.BlockSpec(memory_space=pltpu.VMEM)
    vmem = pltpu.VMEM
    return pl.pallas_call(
        attend_kernel,
        out_shape=jax.ShapeDtypeStruct((4, ROWS // 2, 128), BF16),
        grid_spec=pltpu.PrefetchScalarGridSpec(
            num_scalar_prefetch=1,
            grid=(),
            in_specs=[whole] * 3,
            out_specs=whole,
            scratch_shapes=[
                vmem((17, BLOCK, 128), F32),
                vmem((2, UNROLL, BLOCK, 2 * BLOCK), F32),
                vmem((NB, BLOCK, BLOCK), F32),
            ],
        ),
        compiler_params=pltpu.CompilerParams(vmem_limit_bytes=24 << 20),
        name="attend",
    )(lists, kv, ones_v, qz)


def return_kernel(att_ref, all_ref, send_sems, recv_sems, c_send, c_recv):
    y, z, x_lo, x_hi, core = place()
    me_ctx = ctx_of(y, z, x_lo)
    stays = x_lo == core
    twin = (me_ctx, x_hi * 2 + 1 - core)
    me_global = (x_hi * 2 + x_lo) * 4 + y
    near = [(ctx_of((y + d) % NY, z, core), x_hi * 2 + x_lo) for d in range(4)]
    cross = [(ctx_of((y + d) % NY, z, core), (1 - x_hi) * 2 + x_lo) for d in range(4)]

    barrier = pltpu.get_barrier_semaphore()
    for peer in [twin, *cross, *near[1:]]:
        pl.semaphore_signal(barrier, inc=1, device_id=peer, device_id_type=MESH)

    @pl.when(jnp.logical_not(stays))
    def _():
        pl.semaphore_signal(barrier, inc=1, device_id=near[0], device_id_type=MESH)

    pl.semaphore_wait(barrier, 8 + (x_lo + core) % 2)

    def remote(src, dst, send_sem, recv_sem, device):
        return pltpu.make_async_remote_copy(
            src_ref=src, dst_ref=dst, send_sem=send_sem, recv_sem=recv_sem, device_id=device, device_id_type=MESH
        )

    sent = []

    def send(src, dst, send_sem, recv_sem, device):
        copy = remote(src, dst, send_sem, recv_sem, device)
        copy.start()
        sent.append(copy)

    def send_near(d):
        send(att_ref.at[(y + d) % NY], all_ref.at[me_global], send_sems.at[d], recv_sems.at[d], near[d])

    def send_cross(d):
        send(att_ref.at[(y + d) % NY], all_ref.at[me_global], send_sems.at[4 + d], recv_sems.at[4 + d], cross[d])

    here = remote(att_ref.at[y], all_ref.at[me_global], send_sems.at[0], recv_sems.at[0], near[0])
    local = pltpu.make_async_copy(att_ref.at[y], all_ref.at[me_global], recv_sems.at[0])
    send_cross(2)
    send_cross(1)
    send_cross(3)
    send_near(2)
    send_cross(0)
    send_near(1)
    send_near(3)

    @pl.when(stays)
    def _():
        local.start()

    @pl.when(jnp.logical_not(stays))
    def _():
        here.start()

    def of(source_hi, source_lo, d):
        return all_ref.at[(source_hi * 2 + source_lo) * 4 + (y + NY - d) % NY]

    for d in (0, 1, 3, 2):
        got = of(x_hi, core, d)
        if d == 0:
            @pl.when(stays)
            def _():
                local.wait()

            @pl.when(jnp.logical_not(stays))
            def _():
                here.wait_recv()
        else:
            remote(got, got, send_sems.at[d], recv_sems.at[d], near[d]).wait_recv()
        send(got, got, c_send.at[d], c_recv.at[d], twin)
    for d in (0, 1, 3, 2):
        got = of(1 - x_hi, core, d)
        remote(got, got, send_sems.at[4 + d], recv_sems.at[4 + d], cross[d]).wait_recv()
        send(got, got, c_send.at[4 + d], c_recv.at[4 + d], twin)
    for d in (0, 1, 3, 2):
        got = of(x_hi, 1 - core, d)
        remote(got, got, c_send.at[d], c_recv.at[d], twin).wait_recv()
    for d in (0, 1, 3, 2):
        got = of(1 - x_hi, 1 - core, d)
        remote(got, got, c_send.at[4 + d], c_recv.at[4 + d], twin).wait_recv()

    @pl.when(jnp.logical_not(stays))
    def _():
        here.wait_send()

    for copy in sent:
        copy.wait_send()


def give_back(attended):
    anywhere = pl.BlockSpec(memory_space=pl.ANY)
    dma = pltpu.SemaphoreType.DMA
    return pl.pallas_call(
        return_kernel,
        out_shape=jax.ShapeDtypeStruct((16, ROWS // 2, 128), BF16),
        in_specs=[anywhere],
        out_specs=anywhere,
        scratch_shapes=[dma((8,)), dma((8,)), dma((8,)), dma((8,))],
        compiler_params=pltpu.CompilerParams(collective_id=1, has_side_effects=True, vmem_limit_bytes=16 << 20),
        name="give_back",
    )(attended)


def mix_kernel(att_ref, w_ref, out_ref):
    w = w_ref[...]
    half = ROWS // 2
    for side in range(2):
        cols = slice(side * HEAD_DIM, (side + 1) * HEAD_DIM)
        a = jnp.concatenate([att_ref[g][:, cols] for g in range(16)], axis=1)
        out_ref[side * half : (side + 1) * half, :] = jnp.dot(a, w, preferred_element_type=F32).astype(BF16)


def mix(attended, w_cols):
    whole = pl.BlockSpec(memory_space=pltpu.VMEM)
    return pl.pallas_call(
        mix_kernel,
        out_shape=jax.ShapeDtypeStruct((ROWS, 256), BF16),
        in_specs=[whole, whole],
        out_specs=whole,
        compiler_params=pltpu.CompilerParams(vmem_limit_bytes=16 << 20),
        name="mix",
    )(attended, w_cols)


def body(tokens, w_query, w_key, w_value, w_out, block_mask, block_order):
    kv, ones_v, w_all, lists, qz = exchange(
        tokens, w_query, w_key, w_value, w_out, block_mask, block_order.reshape(1, NB)
    )
    attended = attend(lists, kv.reshape(32 * ROWS, 128), ones_v, qz)
    everything = give_back(attended)
    return mix(everything, w_all.reshape(1024, 256))


def solution(mesh):
    placed = (P("ctx", None), P(None, "head"), P(None, "head"), P(None, "head"), P("head", None), P(), P())
    return jax.shard_map(body, mesh=mesh, in_specs=placed, out_specs=P("ctx", "head"), check_vma=False)
```

```python
import functools

import jax
import jax.numpy as jnp
from jax import lax
from jax.experimental import pallas as pl
from jax.experimental.pallas import tpu as pltpu
from jax.sharding import PartitionSpec as P

HEAD_DIM = 64
BLOCK = 128
NB = 128
ROWS = 512
NY, NZ = 4, 4
LIST_PAD = -1e30
MESH = pl.DeviceIdType.MESH
BF16 = jnp.bfloat16
F32 = jnp.float32


def place():
    ctx = lax.axis_index("ctx")
    head = lax.axis_index("head")
    return ctx // 8, (ctx // 2) % 4, ctx % 2, head // 2, head % 2


def ctx_of(y, z, x_lo):
    return (y * NZ + z) * 2 + x_lo


def write_lists(mask, order_row, z, core, lists_ref):
    sub = lax.broadcasted_iota(jnp.int32, (NB, NB), 0)
    lane = lax.broadcasted_iota(jnp.int32, (NB, NB), 1)
    nt = (((1,), (1,)), ((), ()))

    def as_bf16(condition):
        return condition.astype(F32).astype(BF16)

    initial_of = as_bf16(order_row == sub)
    mine = ((sub // 4 * NZ + z) * 2 + core) * 4 + sub % 4
    row_pick = as_bf16(jnp.logical_and(lane == mine, sub < 16))
    rows_initial = lax.dot_general(row_pick, initial_of, nt, preferred_element_type=F32).astype(BF16)
    mask_rows = jnp.dot(rows_initial, mask.astype(F32).astype(BF16), preferred_element_type=F32).astype(BF16)
    allowed = jnp.dot(mask_rows, initial_of, preferred_element_type=F32)
    rank = jnp.dot(allowed.astype(BF16), as_bf16(sub < lane), preferred_element_type=F32)
    rank = jnp.where(allowed > 0.5, rank, -1.0)
    sub_f = sub.astype(F32)
    lane_row = lax.broadcasted_iota(jnp.int32, (8, NB), 1).astype(F32).astype(BF16)
    for i in range(16):
        hot = as_bf16(rank[i : i + 1, :] == sub_f)
        got = lax.dot_general(lane_row, hot, nt, preferred_element_type=F32)
        lists_ref[i : i + 1, :] = got[0:1, :].astype(jnp.int32)
    ones = jnp.ones((8, NB), BF16)
    count = lax.dot_general(ones, allowed.astype(BF16), nt, preferred_element_type=F32)
    steps = jnp.floor((count + 1.0) * 0.5)
    total = jnp.sum(steps, axis=1, keepdims=True)
    counts = jnp.where(lane[0:8] == 32, total, count).astype(jnp.int32)
    lists_ref[16:32, :] = jnp.zeros((16, NB), jnp.int32)
    lists_ref[17:18, :] = counts[0:1]


def query_place(i):
    b = i % 4
    return i // 4, slice(b % 2 * BLOCK, (b % 2 + 1) * BLOCK), slice(b // 2 * HEAD_DIM, (b // 2 + 1) * HEAD_DIM)


def exchange_kernel(tok_hbm, wq_hbm, wk_hbm, wv_hbm, w_ref, mask_hbm, order_hbm,
                    kv_all, ones_v, w_all, lists_ref, qz,
                    tok_ref, wq_ref, wk_ref, wv_ref, mask_ref, order_ref, kv_ref, q_ref, q_all, in_sems,
                    a_send, a_recv, q_send, q_recv, w_send, w_recv, z_send, z_recv, c_send, c_recv):
    loads = [
        pltpu.make_async_copy(src, dst, in_sems.at[n])
        for n, (src, dst) in enumerate(
            [(wk_hbm, wk_ref), (tok_hbm, tok_ref), (wv_hbm, wv_ref), (wq_hbm, wq_ref), (mask_hbm, mask_ref), (order_hbm, order_ref)]
        )
    ]
    for load in loads:
        load.start()
    y, z, x_lo, x_hi, core = place()
    me_ctx = ctx_of(y, z, x_lo)
    me_head = x_hi * 2 + core
    swap_head = x_hi * 2 + x_lo
    stays = x_lo == core
    up = (ctx_of(y, (z + 1) % NZ, x_lo), me_head)
    down = (ctx_of(y, (z + 3) % NZ, x_lo), me_head)
    twin = (me_ctx, x_hi * 2 + 1 - core)
    head_peers = [(me_ctx, (me_head + k) % 4) for k in range(1, 4)]
    a_to = [(ctx_of((y + d) % NY, z, core), swap_head) for d in range(4)]

    barrier = pltpu.get_barrier_semaphore()
    for peer in [up, down, *head_peers, *a_to[1:]]:
        pl.semaphore_signal(barrier, inc=1, device_id=peer, device_id_type=MESH)

    @pl.when(jnp.logical_not(stays))
    def _():
        pl.semaphore_signal(barrier, inc=1, device_id=a_to[0], device_id_type=MESH)

    half = ROWS // 2
    columns = [slice(j * HEAD_DIM, (j + 1) * HEAD_DIM) for j in range(4)]
    loads[0].wait()
    loads[1].wait()
    tok = tok_ref[...]
    keys = jnp.dot(tok, wk_ref[...], preferred_element_type=F32).astype(BF16)
    loads[2].wait()
    vals = jnp.dot(tok, wv_ref[...], preferred_element_type=F32).astype(BF16)
    for j in range(4):
        kv_ref[j] = jnp.concatenate([keys[:, columns[j]], vals[:, columns[j]]], axis=1)

    pl.semaphore_wait(barrier, 8 + (x_lo + core) % 2)

    def remote(src, dst, send_sem, recv_sem, device):
        return pltpu.make_async_remote_copy(
            src_ref=src, dst_ref=dst, send_sem=send_sem, recv_sem=recv_sem, device_id=device, device_id_type=MESH
        )

    sent = []

    def send(src, dst, send_sem, recv_sem, device):
        copy = remote(src, dst, send_sem, recv_sem, device)
        copy.start()
        sent.append(copy)

    def arrived(dst, send_sem, recv_sem, device):
        remote(dst, dst, send_sem, recv_sem, device).wait_recv()

    own = y % NY
    kv_here = remote(kv_ref.at[own], kv_all.at[me_ctx], a_send.at[0], a_recv.at[0], a_to[0])
    q_here = remote(q_ref.at[own], q_all.at[y], q_send.at[0], q_recv.at[0], a_to[0])
    kv_local = pltpu.make_async_copy(kv_ref.at[own], kv_all.at[me_ctx], a_recv.at[0])
    q_local = pltpu.make_async_copy(q_ref.at[own], q_all.at[y], q_recv.at[0])

    def send_kv(d):
        send(kv_ref.at[(y + d) % NY], kv_all.at[me_ctx], a_send.at[d], a_recv.at[d], a_to[d])

    def send_q(d):
        send(q_ref.at[(y + d) % NY], q_all.at[y], q_send.at[d], q_recv.at[d], a_to[d])

    def chunk(d, dz):
        return kv_all.at[ctx_of((y + NY - d) % NY, (z + NZ + dz) % NZ, core)]

    def pass_on(d):
        send(chunk(d, 0), chunk(d, 0), z_send.at[d], z_recv.at[d], up)
        send(chunk(d, 0), chunk(d, 0), z_send.at[4 + d], z_recv.at[4 + d], down)
        send(chunk(d, 0), chunk(d, 0), c_send.at[d], c_recv.at[d], twin)

    def from_near(d):
        below, above = chunk(d, -1), chunk(d, 1)
        arrived(below, z_send.at[d], z_recv.at[d], up)
        if d in (0, 1):
            send(below, below, z_send.at[8 + d], z_recv.at[8 + d], up)
        send(below, below, c_send.at[4 + d], c_recv.at[4 + d], twin)
        arrived(above, z_send.at[4 + d], z_recv.at[4 + d], down)
        if d in (2, 3):
            send(above, above, z_send.at[8 + d], z_recv.at[8 + d], down)
        send(above, above, c_send.at[8 + d], c_recv.at[8 + d], twin)

    order = (1, 3, 2)
    onward = [(z_send.at[0], z_recv.at[0], up), (z_send.at[4], z_recv.at[4], down), (c_send.at[0], c_recv.at[0], twin)]

    @pl.when(stays)
    def _():
        for send_sem, recv_sem, device in onward:
            remote(kv_ref.at[own], kv_all.at[me_ctx], send_sem, recv_sem, device).start()
        kv_local.start()

    @pl.when(jnp.logical_not(stays))
    def _():
        kv_here.start()

    send_kv(1)
    send_kv(3)
    send_kv(2)

    @pl.when(jnp.logical_not(stays))
    def _():
        kv_here.wait_recv()
        for send_sem, recv_sem, device in onward:
            remote(chunk(0, 0), chunk(0, 0), send_sem, recv_sem, device).start()

    for send_sem, recv_sem, device in onward:
        sent.append(remote(chunk(0, 0), chunk(0, 0), send_sem, recv_sem, device))
    loads[3].wait()
    query = jnp.dot(tok, wq_ref[...], preferred_element_type=F32).astype(BF16)
    for j in range(4):
        q_ref[j] = jnp.concatenate([query[:half, columns[j]], query[half:, columns[j]]], axis=1)

    @pl.when(stays)
    def _():
        q_local.start()

    @pl.when(jnp.logical_not(stays))
    def _():
        q_here.start()

    for d in order:
        send_q(d)
    arrived(chunk(1, 0), a_send.at[1], a_recv.at[1], a_to[1])
    pass_on(1)
    arrived(chunk(3, 0), a_send.at[3], a_recv.at[3], a_to[3])
    pass_on(3)
    arrived(chunk(2, 0), a_send.at[2], a_recv.at[2], a_to[2])
    pass_on(2)
    from_near(0)
    for k in range(1, 4):
        to = (me_head + k) % 4
        send(w_ref.at[:, pl.ds(pl.multiple_of(to * 256, 256), 256)], w_all.at[me_head], w_send.at[k - 1], w_recv.at[k - 1],
             head_peers[k - 1])
    w_local = pltpu.make_async_copy(
        w_ref.at[:, pl.ds(pl.multiple_of(me_head * 256, 256), 256)], w_all.at[me_head], w_recv.at[3]
    )
    w_local.start()
    from_near(1)
    loads[4].wait()
    loads[5].wait()
    write_lists(mask_ref[...], order_ref[...], z, core, lists_ref)

    def twin_arrived(d, dz, place_of):
        got = kv_all.at[ctx_of((y + NY - d) % NY, (z + NZ + dz) % NZ, 1 - core)]
        arrived(got, c_send.at[place_of + d], c_recv.at[place_of + d], twin)

    left = lax.broadcasted_iota(jnp.int32, (ROWS, 128), 1) < HEAD_DIM

    def lay_out(d, dz, sides=(0, 1)):
        for side in sides:
            ctx = ctx_of((y + NY - d) % NY, (z + NZ + dz) % NZ, side)
            rows = pl.ds(pl.multiple_of(ctx * ROWS, ROWS), ROWS)
            got = kv_all[ctx]
            ones_v[rows, :] = jnp.where(left, jnp.ones_like(got), got)

    @pl.when(stays)
    def _():
        q_local.wait()
        kv_local.wait()

    @pl.when(jnp.logical_not(stays))
    def _():
        q_here.wait_recv()

    for d in order:
        arrived(q_all.at[(y + NY - d) % NY], q_send.at[d], q_recv.at[d], a_to[d])
    narrow = lax.broadcasted_iota(jnp.int32, (BLOCK, 128), 1) < HEAD_DIM
    for i in range(16):
        step, rows, cols = query_place(i)
        q = q_all[step, rows, :]
        if cols.start:
            q = jnp.concatenate([q[:, HEAD_DIM:], q[:, :HEAD_DIM]], axis=1)
        qz[i] = jnp.where(narrow, q, jnp.zeros_like(q))
    qz[16] = jnp.zeros((BLOCK, 128), BF16)
    for d in (0, 1, 3, 2):
        twin_arrived(d, 0, 0)
        lay_out(d, 0)
    from_near(3)
    from_near(2)
    for d in (0, 1, 3, 2):
        twin_arrived(d, -1, 4)
        twin_arrived(d, 1, 8)
        lay_out(d, -1)
        lay_out(d, 1)
    for d in (0, 1, 3, 2):
        far = chunk(d, 2)
        arrived(far, z_send.at[8 + d], z_recv.at[8 + d], up)
        send(far, far, c_send.at[12 + d], c_recv.at[12 + d], twin)
        lay_out(d, 2, (core,))
    for d in (0, 1, 3, 2):
        twin_arrived(d, 2, 12)
        lay_out(d, 2, (1 - core,))

    @pl.when(jnp.logical_not(stays))
    def _():
        kv_here.wait_send()
        q_here.wait_send()

    for k in range(1, 4):
        arrived(w_all.at[(me_head + 4 - k) % 4], w_send.at[k - 1], w_recv.at[k - 1], head_peers[k - 1])
    w_local.wait()
    for copy in sent:
        copy.wait_send()


def exchange(tokens, w_query, w_key, w_value, w_out, block_mask, order_row):
    in_hbm = pl.BlockSpec(memory_space=pltpu.HBM)
    operands = [tokens, w_query, w_key, w_value, w_out, block_mask, order_row]
    operands = [pltpu.with_memory_space_constraint(a, pltpu.HBM) for a in operands]
    anywhere = pl.BlockSpec(memory_space=pl.ANY)
    dma = pltpu.SemaphoreType.DMA
    vmem = pltpu.VMEM
    in_vmem = pl.BlockSpec(memory_space=vmem)
    return pl.pallas_call(
        exchange_kernel,
        out_shape=(
            jax.ShapeDtypeStruct((32, ROWS, 128), BF16),
            jax.ShapeDtypeStruct((32 * ROWS, 128), BF16),
            jax.ShapeDtypeStruct((4, 256, 256), BF16),
            jax.ShapeDtypeStruct((32, NB), jnp.int32),
            jax.ShapeDtypeStruct((17, BLOCK, 128), BF16),
        ),
        in_specs=[in_hbm] * 7,
        out_specs=(in_vmem, in_vmem, anywhere, in_vmem, in_vmem),
        scratch_shapes=[
            vmem((ROWS, 1024), BF16), vmem((1024, 256), BF16), vmem((1024, 256), BF16), vmem((1024, 256), BF16),
            vmem((NB, NB), jnp.int32), vmem((1, NB), jnp.int32), vmem((4, ROWS, 128), BF16), vmem((4, ROWS // 2, 128), BF16),
            vmem((4, ROWS // 2, 128), BF16), dma((6,)),
            dma((4,)), dma((4,)), dma((4,)), dma((4,)), dma((4,)), dma((4,)),
            dma((12,)), dma((12,)), dma((16,)), dma((16,)),
        ],
        compiler_params=pltpu.CompilerParams(collective_id=0, has_side_effects=True, vmem_limit_bytes=24 << 20),
        name="exchange",
    )(*operands)


UNROLL = 7
EXP2_SCALE = (HEAD_DIM ** -0.5) * 1.4426950408889634
SMALLEST, LARGEST = 1e-20, 1e30
NT = (((1,), (1,)), ((), ()))


def attend_kernel(lists, kv_ref, ones_v, qz, out_ref, acc, sbuf, scores):
    zero = jnp.zeros((BLOCK, 128), F32)
    for i in range(17):
        acc[i] = zero
    second = lax.broadcasted_iota(jnp.int32, (1, 2 * BLOCK), 1) >= BLOCK

    def rows_at(i, k):
        return pl.ds(pl.multiple_of(lists[i, jnp.minimum(k, NB - 1)] * BLOCK, BLOCK), BLOCK)

    def advance(i, k):
        done = k + 2 >= lists[17, i]
        return jnp.minimum(jnp.where(done, i + 1, i), 16), jnp.where(done, 0, k + 2)

    def score(slot, i, k):
        for u in range(UNROLL):
            keys = jnp.concatenate([kv_ref[rows_at(i, k), :], kv_ref[rows_at(i, k + 1), :]], axis=0)
            sbuf[slot, u] = lax.dot_general(qz[i], keys, NT, preferred_element_type=F32)
            i, k = advance(i, k)
        return i, k

    def weigh(slot, i, k):
        for u in range(UNROLL):
            bias = jnp.where(k + 1 < lists[17, i], 0.0, LIST_PAD).astype(F32)
            vals = jnp.concatenate([ones_v[rows_at(i, k), :], ones_v[rows_at(i, k + 1), :]], axis=0)
            p = jnp.exp2(sbuf[slot, u] * EXP2_SCALE + jnp.where(second, bias, 0.0)).astype(BF16)
            acc[i] += jnp.dot(p, vals, preferred_element_type=F32)
            i, k = advance(i, k)

    start = jnp.int32(0)
    i1, k1 = score(0, start, start)

    def step(_, carry):
        i, k, i1, k1 = carry
        i2, k2 = score(1, i1, k1)
        weigh(0, i, k)
        i3, k3 = score(0, i2, k2)
        weigh(1, i1, k1)
        return i2, k2, i3, k3

    lax.fori_loop(0, (lists[17, 32] + 2 * UNROLL - 1) // (2 * UNROLL), step, (start, start, i1, k1))

    fine = jnp.full((BLOCK, HEAD_DIM), 1.0, F32)
    for i in range(16):
        y, rows, cols = query_place(i)
        denom = acc[i][:, :HEAD_DIM]
        within = jnp.logical_and(denom >= SMALLEST, denom <= LARGEST)
        fine = jnp.where(within, fine, 0.0)
        out_ref[y, rows, cols] = (acc[i][:, HEAD_DIM:] / denom).astype(BF16)

    @pl.when(jnp.min(fine) < 0.5)
    def _():
        for i in range(16):
            y, rows, cols = query_place(i)
            n = lists[17, i]

            def first(k, top):
                s = lax.dot_general(qz[i], kv_ref[rows_at(i, k), :], NT, preferred_element_type=F32)
                scores[k] = s
                return jnp.maximum(top, s)

            top = lax.fori_loop(0, n, first, jnp.full((BLOCK, BLOCK), -3e38, F32))
            top = jnp.max(top, axis=1, keepdims=True)

            def then(k, carry):
                total, weighted = carry
                p = jnp.exp2((scores[k] - top) * EXP2_SCALE)
                return total + p, weighted + jnp.dot(
                    p.astype(BF16), kv_ref[rows_at(i, k), :], preferred_element_type=F32
                )

            total, weighted = lax.fori_loop(0, n, then, (zero, zero))
            denom = jnp.sum(total, axis=1, keepdims=True)
            out_ref[y, rows, cols] = (weighted[:, HEAD_DIM:] / denom).astype(BF16)


def attend(lists, kv, ones_v, qz):
    whole = pl.BlockSpec(memory_space=pltpu.VMEM)
    vmem = pltpu.VMEM
    return pl.pallas_call(
        attend_kernel,
        out_shape=jax.ShapeDtypeStruct((4, ROWS // 2, 128), BF16),
        grid_spec=pltpu.PrefetchScalarGridSpec(
            num_scalar_prefetch=1,
            grid=(),
            in_specs=[whole] * 3,
            out_specs=whole,
            scratch_shapes=[
                vmem((17, BLOCK, 128), F32),
                vmem((2, UNROLL, BLOCK, 2 * BLOCK), F32),
                vmem((NB, BLOCK, BLOCK), F32),
            ],
        ),
        compiler_params=pltpu.CompilerParams(vmem_limit_bytes=24 << 20),
        name="attend",
    )(lists, kv, ones_v, qz)


def return_kernel(att_ref, all_ref, send_sems, recv_sems, c_send, c_recv):
    y, z, x_lo, x_hi, core = place()
    me_ctx = ctx_of(y, z, x_lo)
    stays = x_lo == core
    twin = (me_ctx, x_hi * 2 + 1 - core)
    me_global = (x_hi * 2 + x_lo) * 4 + y
    near = [(ctx_of((y + d) % NY, z, core), x_hi * 2 + x_lo) for d in range(4)]
    cross = [(ctx_of((y + d) % NY, z, core), (1 - x_hi) * 2 + x_lo) for d in range(4)]

    barrier = pltpu.get_barrier_semaphore()
    for peer in [twin, *cross, *near[1:]]:
        pl.semaphore_signal(barrier, inc=1, device_id=peer, device_id_type=MESH)

    @pl.when(jnp.logical_not(stays))
    def _():
        pl.semaphore_signal(barrier, inc=1, device_id=near[0], device_id_type=MESH)

    pl.semaphore_wait(barrier, 8 + (x_lo + core) % 2)

    def remote(src, dst, send_sem, recv_sem, device):
        return pltpu.make_async_remote_copy(
            src_ref=src, dst_ref=dst, send_sem=send_sem, recv_sem=recv_sem, device_id=device, device_id_type=MESH
        )

    sent = []

    def send(src, dst, send_sem, recv_sem, device):
        copy = remote(src, dst, send_sem, recv_sem, device)
        copy.start()
        sent.append(copy)

    def send_near(d):
        send(att_ref.at[(y + d) % NY], all_ref.at[me_global], send_sems.at[d], recv_sems.at[d], near[d])

    def send_cross(d):
        send(att_ref.at[(y + d) % NY], all_ref.at[me_global], send_sems.at[4 + d], recv_sems.at[4 + d], cross[d])

    here = remote(att_ref.at[y], all_ref.at[me_global], send_sems.at[0], recv_sems.at[0], near[0])
    local = pltpu.make_async_copy(att_ref.at[y], all_ref.at[me_global], recv_sems.at[0])
    send_cross(2)
    send_cross(1)
    send_cross(3)
    send_near(2)
    send_cross(0)
    send_near(1)
    send_near(3)

    @pl.when(stays)
    def _():
        local.start()

    @pl.when(jnp.logical_not(stays))
    def _():
        here.start()

    def of(source_hi, source_lo, d):
        return all_ref.at[(source_hi * 2 + source_lo) * 4 + (y + NY - d) % NY]

    def near_in(d):
        got = of(x_hi, core, d)
        if d == 0:
            @pl.when(stays)
            def _():
                local.wait()

            @pl.when(jnp.logical_not(stays))
            def _():
                here.wait_recv()
        else:
            remote(got, got, send_sems.at[d], recv_sems.at[d], near[d]).wait_recv()
        send(got, got, c_send.at[d], c_recv.at[d], twin)

    def cross_in(d):
        got = of(1 - x_hi, core, d)
        remote(got, got, send_sems.at[4 + d], recv_sems.at[4 + d], cross[d]).wait_recv()
        send(got, got, c_send.at[4 + d], c_recv.at[4 + d], twin)

    near_in(0)
    cross_in(0)
    cross_in(1)
    cross_in(3)
    near_in(1)
    near_in(3)
    near_in(2)
    cross_in(2)
    for d in (0, 1, 3, 2):
        got = of(x_hi, 1 - core, d)
        remote(got, got, c_send.at[d], c_recv.at[d], twin).wait_recv()
    for d in (0, 1, 3, 2):
        got = of(1 - x_hi, 1 - core, d)
        remote(got, got, c_send.at[4 + d], c_recv.at[4 + d], twin).wait_recv()

    @pl.when(jnp.logical_not(stays))
    def _():
        here.wait_send()

    for copy in sent:
        copy.wait_send()


def give_back(attended):
    anywhere = pl.BlockSpec(memory_space=pl.ANY)
    dma = pltpu.SemaphoreType.DMA
    return pl.pallas_call(
        return_kernel,
        out_shape=jax.ShapeDtypeStruct((16, ROWS // 2, 128), BF16),
        in_specs=[anywhere],
        out_specs=anywhere,
        scratch_shapes=[dma((8,)), dma((8,)), dma((8,)), dma((8,))],
        compiler_params=pltpu.CompilerParams(collective_id=1, has_side_effects=True, vmem_limit_bytes=16 << 20),
        name="give_back",
    )(attended)


def mix_kernel(att_ref, w_ref, out_ref):
    w = w_ref[...]
    half = ROWS // 2
    for side in range(2):
        cols = slice(side * HEAD_DIM, (side + 1) * HEAD_DIM)
        a = jnp.concatenate([att_ref[g][:, cols] for g in range(16)], axis=1)
        out_ref[side * half : (side + 1) * half, :] = jnp.dot(a, w, preferred_element_type=F32).astype(BF16)


def mix(attended, w_cols):
    whole = pl.BlockSpec(memory_space=pltpu.VMEM)
    return pl.pallas_call(
        mix_kernel,
        out_shape=jax.ShapeDtypeStruct((ROWS, 256), BF16),
        in_specs=[whole, whole],
        out_specs=whole,
        compiler_params=pltpu.CompilerParams(vmem_limit_bytes=16 << 20),
        name="mix",
    )(attended, w_cols)


def body(tokens, w_query, w_key, w_value, w_out, block_mask, block_order):
    kv, ones_v, w_all, lists, qz = exchange(
        tokens, w_query, w_key, w_value, w_out, block_mask, block_order.reshape(1, NB)
    )
    attended = attend(lists, kv.reshape(32 * ROWS, 128), ones_v, qz)
    everything = give_back(attended)
    return mix(everything, w_all.reshape(1024, 256))


def solution(mesh):
    placed = (P("ctx", None), P(None, "head"), P(None, "head"), P(None, "head"), P("head", None), P(), P())
    return jax.shard_map(body, mesh=mesh, in_specs=placed, out_specs=P("ctx", "head"), check_vma=False)
```

```python
import functools

import jax
import jax.numpy as jnp
from jax import lax
from jax.experimental import pallas as pl
from jax.experimental.pallas import tpu as pltpu
from jax.sharding import PartitionSpec as P

HEAD_DIM = 64
BLOCK = 128
NB = 128
ROWS = 512
NY, NZ = 4, 4
LIST_PAD = -1e30
MESH = pl.DeviceIdType.MESH
BF16 = jnp.bfloat16
F32 = jnp.float32


def place():
    ctx = lax.axis_index("ctx")
    head = lax.axis_index("head")
    return ctx // 8, (ctx // 2) % 4, ctx % 2, head // 2, head % 2


def ctx_of(y, z, x_lo):
    return (y * NZ + z) * 2 + x_lo


def write_lists(mask, order_row, z, core, lists_ref):
    sub = lax.broadcasted_iota(jnp.int32, (NB, NB), 0)
    lane = lax.broadcasted_iota(jnp.int32, (NB, NB), 1)
    nt = (((1,), (1,)), ((), ()))

    def as_bf16(condition):
        return condition.astype(F32).astype(BF16)

    initial_of = as_bf16(order_row == sub)
    mine = ((sub // 4 * NZ + z) * 2 + core) * 4 + sub % 4
    row_pick = as_bf16(jnp.logical_and(lane == mine, sub < 16))
    rows_initial = lax.dot_general(row_pick, initial_of, nt, preferred_element_type=F32).astype(BF16)
    mask_rows = jnp.dot(rows_initial, mask.astype(F32).astype(BF16), preferred_element_type=F32).astype(BF16)
    allowed = jnp.dot(mask_rows, initial_of, preferred_element_type=F32)
    rank = jnp.dot(allowed.astype(BF16), as_bf16(sub < lane), preferred_element_type=F32)
    rank = jnp.where(allowed > 0.5, rank, -1.0)
    sub_f = sub.astype(F32)
    lane_row = lax.broadcasted_iota(jnp.int32, (8, NB), 1).astype(F32).astype(BF16)
    for i in range(16):
        hot = as_bf16(rank[i : i + 1, :] == sub_f)
        got = lax.dot_general(lane_row, hot, nt, preferred_element_type=F32)
        lists_ref[i : i + 1, :] = got[0:1, :].astype(jnp.int32)
    ones = jnp.ones((8, NB), BF16)
    count = lax.dot_general(ones, allowed.astype(BF16), nt, preferred_element_type=F32)
    steps = jnp.floor((count + 1.0) * 0.5)
    total = jnp.sum(steps, axis=1, keepdims=True)
    counts = jnp.where(lane[0:8] == 32, total, count).astype(jnp.int32)
    lists_ref[16:32, :] = jnp.zeros((16, NB), jnp.int32)
    lists_ref[17:18, :] = counts[0:1]


def query_place(i):
    b = i % 4
    return i // 4, slice(b % 2 * BLOCK, (b % 2 + 1) * BLOCK), slice(b // 2 * HEAD_DIM, (b // 2 + 1) * HEAD_DIM)


def exchange_kernel(tok_hbm, wq_hbm, wk_hbm, wv_hbm, w_ref, mask_hbm, order_hbm,
                    kv_all, ones_v, w_all, lists_ref, qz,
                    tok_ref, wq_ref, wk_ref, wv_ref, mask_ref, order_ref, kv_ref, q_ref, q_all, in_sems,
                    a_send, a_recv, q_send, q_recv, w_send, w_recv, z_send, z_recv, c_send, c_recv):
    loads = [
        pltpu.make_async_copy(src, dst, in_sems.at[n])
        for n, (src, dst) in enumerate(
            [(wk_hbm, wk_ref), (tok_hbm, tok_ref), (wv_hbm, wv_ref), (wq_hbm, wq_ref), (mask_hbm, mask_ref), (order_hbm, order_ref)]
        )
    ]
    for load in loads:
        load.start()
    y, z, x_lo, x_hi, core = place()
    me_ctx = ctx_of(y, z, x_lo)
    me_head = x_hi * 2 + core
    swap_head = x_hi * 2 + x_lo
    stays = x_lo == core
    up = (ctx_of(y, (z + 1) % NZ, x_lo), me_head)
    down = (ctx_of(y, (z + 3) % NZ, x_lo), me_head)
    twin = (me_ctx, x_hi * 2 + 1 - core)
    head_peers = [(me_ctx, (me_head + k) % 4) for k in range(1, 4)]
    a_to = [(ctx_of((y + d) % NY, z, core), swap_head) for d in range(4)]

    barrier = pltpu.get_barrier_semaphore()
    for peer in [up, down, *head_peers, *a_to[1:]]:
        pl.semaphore_signal(barrier, inc=1, device_id=peer, device_id_type=MESH)

    @pl.when(jnp.logical_not(stays))
    def _():
        pl.semaphore_signal(barrier, inc=1, device_id=a_to[0], device_id_type=MESH)

    half = ROWS // 2
    columns = [slice(j * HEAD_DIM, (j + 1) * HEAD_DIM) for j in range(4)]
    loads[0].wait()
    loads[1].wait()
    tok = tok_ref[...]
    keys = jnp.dot(tok, wk_ref[...], preferred_element_type=F32).astype(BF16)
    loads[2].wait()
    vals = jnp.dot(tok, wv_ref[...], preferred_element_type=F32).astype(BF16)
    for j in range(4):
        kv_ref[j] = jnp.concatenate([keys[:, columns[j]], vals[:, columns[j]]], axis=1)

    pl.semaphore_wait(barrier, 8 + (x_lo + core) % 2)

    def remote(src, dst, send_sem, recv_sem, device):
        return pltpu.make_async_remote_copy(
            src_ref=src, dst_ref=dst, send_sem=send_sem, recv_sem=recv_sem, device_id=device, device_id_type=MESH
        )

    sent = []

    def send(src, dst, send_sem, recv_sem, device):
        copy = remote(src, dst, send_sem, recv_sem, device)
        copy.start()
        sent.append(copy)

    def arrived(dst, send_sem, recv_sem, device):
        remote(dst, dst, send_sem, recv_sem, device).wait_recv()

    own = y % NY
    kv_here = remote(kv_ref.at[own], kv_all.at[me_ctx], a_send.at[0], a_recv.at[0], a_to[0])
    q_here = remote(q_ref.at[own], q_all.at[y], q_send.at[0], q_recv.at[0], a_to[0])
    kv_local = pltpu.make_async_copy(kv_ref.at[own], kv_all.at[me_ctx], a_recv.at[0])
    q_local = pltpu.make_async_copy(q_ref.at[own], q_all.at[y], q_recv.at[0])

    def send_kv(d):
        send(kv_ref.at[(y + d) % NY], kv_all.at[me_ctx], a_send.at[d], a_recv.at[d], a_to[d])

    def send_q(d):
        send(q_ref.at[(y + d) % NY], q_all.at[y], q_send.at[d], q_recv.at[d], a_to[d])

    def chunk(d, dz):
        return kv_all.at[ctx_of((y + NY - d) % NY, (z + NZ + dz) % NZ, core)]

    def pass_on(d):
        send(chunk(d, 0), chunk(d, 0), z_send.at[d], z_recv.at[d], up)
        send(chunk(d, 0), chunk(d, 0), z_send.at[4 + d], z_recv.at[4 + d], down)
        send(chunk(d, 0), chunk(d, 0), c_send.at[d], c_recv.at[d], twin)

    def from_near(d):
        below, above = chunk(d, -1), chunk(d, 1)
        arrived(below, z_send.at[d], z_recv.at[d], up)
        if d in (0, 1):
            send(below, below, z_send.at[8 + d], z_recv.at[8 + d], up)
        send(below, below, c_send.at[4 + d], c_recv.at[4 + d], twin)
        arrived(above, z_send.at[4 + d], z_recv.at[4 + d], down)
        if d in (2, 3):
            send(above, above, z_send.at[8 + d], z_recv.at[8 + d], down)
        send(above, above, c_send.at[8 + d], c_recv.at[8 + d], twin)

    order = (1, 3, 2)
    onward = [(z_send.at[0], z_recv.at[0], up), (z_send.at[4], z_recv.at[4], down), (c_send.at[0], c_recv.at[0], twin)]

    @pl.when(stays)
    def _():
        for send_sem, recv_sem, device in onward:
            remote(kv_ref.at[own], kv_all.at[me_ctx], send_sem, recv_sem, device).start()
        kv_local.start()

    @pl.when(jnp.logical_not(stays))
    def _():
        kv_here.start()

    send_kv(1)
    send_kv(3)
    send_kv(2)

    @pl.when(jnp.logical_not(stays))
    def _():
        kv_here.wait_recv()
        for send_sem, recv_sem, device in onward:
            remote(chunk(0, 0), chunk(0, 0), send_sem, recv_sem, device).start()

    for send_sem, recv_sem, device in onward:
        sent.append(remote(chunk(0, 0), chunk(0, 0), send_sem, recv_sem, device))
    loads[3].wait()
    query = jnp.dot(tok, wq_ref[...], preferred_element_type=F32).astype(BF16)
    for j in range(4):
        q_ref[j] = jnp.concatenate([query[:half, columns[j]], query[half:, columns[j]]], axis=1)

    @pl.when(stays)
    def _():
        q_local.start()

    @pl.when(jnp.logical_not(stays))
    def _():
        q_here.start()

    for d in order:
        send_q(d)
    arrived(chunk(1, 0), a_send.at[1], a_recv.at[1], a_to[1])
    pass_on(1)
    arrived(chunk(3, 0), a_send.at[3], a_recv.at[3], a_to[3])
    pass_on(3)
    arrived(chunk(2, 0), a_send.at[2], a_recv.at[2], a_to[2])
    pass_on(2)
    from_near(0)
    for k in range(1, 4):
        to = (me_head + k) % 4
        send(w_ref.at[:, pl.ds(pl.multiple_of(to * 256, 256), 256)], w_all.at[me_head], w_send.at[k - 1], w_recv.at[k - 1],
             head_peers[k - 1])
    w_local = pltpu.make_async_copy(
        w_ref.at[:, pl.ds(pl.multiple_of(me_head * 256, 256), 256)], w_all.at[me_head], w_recv.at[3]
    )
    w_local.start()
    from_near(1)
    loads[4].wait()
    loads[5].wait()
    write_lists(mask_ref[...], order_ref[...], z, core, lists_ref)

    def twin_arrived(d, dz, place_of):
        got = kv_all.at[ctx_of((y + NY - d) % NY, (z + NZ + dz) % NZ, 1 - core)]
        arrived(got, c_send.at[place_of + d], c_recv.at[place_of + d], twin)

    def lay_out(d, dz, sides=(0, 1)):
        for side in sides:
            ctx = ctx_of((y + NY - d) % NY, (z + NZ + dz) % NZ, side)
            for b in range(ROWS // BLOCK):
                got = kv_all[ctx, b * BLOCK : (b + 1) * BLOCK, :].astype(F32)
                ones_v[ctx * 4 + b, 16:80, :] = jnp.transpose(got)[HEAD_DIM:, :].astype(BF16)

    def ones_of(block, _):
        ones_v[block, 0:16, :] = jnp.ones((16, 128), BF16)
        return 0

    lax.fori_loop(0, NB, ones_of, 0)

    @pl.when(stays)
    def _():
        q_local.wait()
        kv_local.wait()

    @pl.when(jnp.logical_not(stays))
    def _():
        q_here.wait_recv()

    for d in order:
        arrived(q_all.at[(y + NY - d) % NY], q_send.at[d], q_recv.at[d], a_to[d])
    narrow = lax.broadcasted_iota(jnp.int32, (BLOCK, 128), 1) < HEAD_DIM
    for i in range(16):
        step, rows, cols = query_place(i)
        q = q_all[step, rows, :]
        if cols.start:
            q = jnp.concatenate([q[:, HEAD_DIM:], q[:, :HEAD_DIM]], axis=1)
        qz[i] = jnp.where(narrow, q, jnp.zeros_like(q))
    qz[16] = jnp.zeros((BLOCK, 128), BF16)
    from_near(3)
    from_near(2)
    for d in (0, 1, 3, 2):
        twin_arrived(d, 0, 0)
        lay_out(d, 0)
    for d in (0, 1, 3, 2):
        twin_arrived(d, -1, 4)
        twin_arrived(d, 1, 8)
        lay_out(d, -1)
        lay_out(d, 1)
        far = chunk(d, 2)
        arrived(far, z_send.at[8 + d], z_recv.at[8 + d], up)
        send(far, far, c_send.at[12 + d], c_recv.at[12 + d], twin)
    for d in (0, 1, 3, 2):
        lay_out(d, 2, (core,))
        twin_arrived(d, 2, 12)
        lay_out(d, 2, (1 - core,))

    @pl.when(jnp.logical_not(stays))
    def _():
        kv_here.wait_send()
        q_here.wait_send()

    for k in range(1, 4):
        arrived(w_all.at[(me_head + 4 - k) % 4], w_send.at[k - 1], w_recv.at[k - 1], head_peers[k - 1])
    w_local.wait()
    for copy in sent:
        copy.wait_send()


def exchange(tokens, w_query, w_key, w_value, w_out, block_mask, order_row):
    in_hbm = pl.BlockSpec(memory_space=pltpu.HBM)
    operands = [tokens, w_query, w_key, w_value, w_out, block_mask, order_row]
    operands = [pltpu.with_memory_space_constraint(a, pltpu.HBM) for a in operands]
    anywhere = pl.BlockSpec(memory_space=pl.ANY)
    dma = pltpu.SemaphoreType.DMA
    vmem = pltpu.VMEM
    in_vmem = pl.BlockSpec(memory_space=vmem)
    return pl.pallas_call(
        exchange_kernel,
        out_shape=(
            jax.ShapeDtypeStruct((32, ROWS, 128), BF16),
            jax.ShapeDtypeStruct((NB, 80, BLOCK), BF16),
            jax.ShapeDtypeStruct((4, 256, 256), BF16),
            jax.ShapeDtypeStruct((32, NB), jnp.int32),
            jax.ShapeDtypeStruct((17, BLOCK, 128), BF16),
        ),
        in_specs=[in_hbm] * 7,
        out_specs=(in_vmem, in_vmem, anywhere, in_vmem, in_vmem),
        scratch_shapes=[
            vmem((ROWS, 1024), BF16), vmem((1024, 256), BF16), vmem((1024, 256), BF16), vmem((1024, 256), BF16),
            vmem((NB, NB), jnp.int32), vmem((1, NB), jnp.int32), vmem((4, ROWS, 128), BF16), vmem((4, ROWS // 2, 128), BF16),
            vmem((4, ROWS // 2, 128), BF16), dma((6,)),
            dma((4,)), dma((4,)), dma((4,)), dma((4,)), dma((4,)), dma((4,)),
            dma((12,)), dma((12,)), dma((16,)), dma((16,)),
        ],
        compiler_params=pltpu.CompilerParams(collective_id=0, has_side_effects=True, vmem_limit_bytes=24 << 20),
        name="exchange",
    )(*operands)


UNROLL = 7
EXP2_SCALE = (HEAD_DIM ** -0.5) * 1.4426950408889634
SMALLEST, LARGEST = 1e-20, 1e30
NT = (((1,), (1,)), ((), ()))


def attend_kernel(lists, kv_ref, ones_v, qz, out_ref, acc, sbuf, scores):
    zero = jnp.zeros((BLOCK, 128), F32)
    for i in range(17):
        acc[i] = jnp.zeros((80, BLOCK), F32)
    second = lax.broadcasted_iota(jnp.int32, (2 * BLOCK, 1), 0) >= BLOCK

    def block_at(i, k):
        return lists[i, jnp.minimum(k, NB - 1)]

    def rows_at(i, k):
        return pl.ds(pl.multiple_of(block_at(i, k) * BLOCK, BLOCK), BLOCK)

    def advance(i, k):
        done = k + 2 >= lists[17, i]
        return jnp.minimum(jnp.where(done, i + 1, i), 16), jnp.where(done, 0, k + 2)

    def score(slot, i, k):
        for u in range(UNROLL):
            keys = jnp.concatenate([kv_ref[rows_at(i, k), :], kv_ref[rows_at(i, k + 1), :]], axis=0)
            bias = jnp.where(k + 1 < lists[17, i], 0.0, LIST_PAD).astype(F32)
            s = lax.dot_general(keys, qz[i], NT, preferred_element_type=F32)
            sbuf[slot, u] = jnp.exp2(s * EXP2_SCALE + jnp.where(second, bias, 0.0)).astype(BF16)
            i, k = advance(i, k)
        return i, k

    def weigh(slot, i, k):
        for u in range(UNROLL):
            vals = jnp.concatenate([ones_v[block_at(i, k)], ones_v[block_at(i, k + 1)]], axis=1)
            acc[i] += jnp.dot(vals, sbuf[slot, u], preferred_element_type=F32)
            i, k = advance(i, k)

    start = jnp.int32(0)
    i1, k1 = score(0, start, start)

    def step(_, carry):
        i, k, i1, k1 = carry
        i2, k2 = score(1, i1, k1)
        weigh(0, i, k)
        i3, k3 = score(0, i2, k2)
        weigh(1, i1, k1)
        return i2, k2, i3, k3

    lax.fori_loop(0, (lists[17, 32] + 2 * UNROLL - 1) // (2 * UNROLL), step, (start, start, i1, k1))

    fine = jnp.full((1, BLOCK), 1.0, F32)
    for i in range(16):
        y, rows, cols = query_place(i)
        denom = acc[i][0:1, :]
        within = jnp.logical_and(denom >= SMALLEST, denom <= LARGEST)
        fine = jnp.where(within, fine, 0.0)
        out_ref[y, rows, cols] = jnp.transpose(acc[i][16:80, :] / denom).astype(BF16)

    @pl.when(jnp.min(fine) < 0.5)
    def _():
        for i in range(16):
            y, rows, cols = query_place(i)
            n = lists[17, i]

            def first(k, top):
                s = lax.dot_general(qz[i], kv_ref[rows_at(i, k), :], NT, preferred_element_type=F32)
                scores[k] = s
                return jnp.maximum(top, s)

            top = lax.fori_loop(0, n, first, jnp.full((BLOCK, BLOCK), -3e38, F32))
            top = jnp.max(top, axis=1, keepdims=True)

            def then(k, carry):
                total, weighted = carry
                p = jnp.exp2((scores[k] - top) * EXP2_SCALE)
                return total + p, weighted + jnp.dot(
                    p.astype(BF16), kv_ref[rows_at(i, k), :], preferred_element_type=F32
                )

            total, weighted = lax.fori_loop(0, n, then, (zero, zero))
            denom = jnp.sum(total, axis=1, keepdims=True)
            out_ref[y, rows, cols] = (weighted[:, HEAD_DIM:] / denom).astype(BF16)


def attend(lists, kv, ones_v, qz):
    whole = pl.BlockSpec(memory_space=pltpu.VMEM)
    vmem = pltpu.VMEM
    return pl.pallas_call(
        attend_kernel,
        out_shape=jax.ShapeDtypeStruct((4, ROWS // 2, 128), BF16),
        grid_spec=pltpu.PrefetchScalarGridSpec(
            num_scalar_prefetch=1,
            grid=(),
            in_specs=[whole] * 3,
            out_specs=whole,
            scratch_shapes=[
                vmem((17, 80, BLOCK), F32),
                vmem((2, UNROLL, 2 * BLOCK, BLOCK), BF16),
                vmem((NB, BLOCK, BLOCK), F32),
            ],
        ),
        compiler_params=pltpu.CompilerParams(vmem_limit_bytes=24 << 20),
        name="attend",
    )(lists, kv, ones_v, qz)


def return_kernel(att_ref, all_ref, send_sems, recv_sems, c_send, c_recv):
    y, z, x_lo, x_hi, core = place()
    me_ctx = ctx_of(y, z, x_lo)
    stays = x_lo == core
    twin = (me_ctx, x_hi * 2 + 1 - core)
    me_global = (x_hi * 2 + x_lo) * 4 + y
    near = [(ctx_of((y + d) % NY, z, core), x_hi * 2 + x_lo) for d in range(4)]
    cross = [(ctx_of((y + d) % NY, z, core), (1 - x_hi) * 2 + x_lo) for d in range(4)]

    barrier = pltpu.get_barrier_semaphore()
    for peer in [twin, *cross, *near[1:]]:
        pl.semaphore_signal(barrier, inc=1, device_id=peer, device_id_type=MESH)

    @pl.when(jnp.logical_not(stays))
    def _():
        pl.semaphore_signal(barrier, inc=1, device_id=near[0], device_id_type=MESH)

    pl.semaphore_wait(barrier, 8 + (x_lo + core) % 2)

    def remote(src, dst, send_sem, recv_sem, device):
        return pltpu.make_async_remote_copy(
            src_ref=src, dst_ref=dst, send_sem=send_sem, recv_sem=recv_sem, device_id=device, device_id_type=MESH
        )

    sent = []

    def send(src, dst, send_sem, recv_sem, device):
        copy = remote(src, dst, send_sem, recv_sem, device)
        copy.start()
        sent.append(copy)

    def send_near(d):
        send(att_ref.at[(y + d) % NY], all_ref.at[me_global], send_sems.at[d], recv_sems.at[d], near[d])

    def send_cross(d):
        send(att_ref.at[(y + d) % NY], all_ref.at[me_global], send_sems.at[4 + d], recv_sems.at[4 + d], cross[d])

    here = remote(att_ref.at[y], all_ref.at[me_global], send_sems.at[0], recv_sems.at[0], near[0])
    local = pltpu.make_async_copy(att_ref.at[y], all_ref.at[me_global], recv_sems.at[0])
    send_cross(2)
    send_cross(1)
    send_cross(3)
    send_near(2)
    send_cross(0)
    send_near(1)
    send_near(3)

    @pl.when(stays)
    def _():
        local.start()

    @pl.when(jnp.logical_not(stays))
    def _():
        here.start()

    def of(source_hi, source_lo, d):
        return all_ref.at[(source_hi * 2 + source_lo) * 4 + (y + NY - d) % NY]

    def near_in(d):
        got = of(x_hi, core, d)
        if d == 0:
            @pl.when(stays)
            def _():
                local.wait()

            @pl.when(jnp.logical_not(stays))
            def _():
                here.wait_recv()
        else:
            remote(got, got, send_sems.at[d], recv_sems.at[d], near[d]).wait_recv()
        send(got, got, c_send.at[d], c_recv.at[d], twin)

    def cross_in(d):
        got = of(1 - x_hi, core, d)
        remote(got, got, send_sems.at[4 + d], recv_sems.at[4 + d], cross[d]).wait_recv()
        send(got, got, c_send.at[4 + d], c_recv.at[4 + d], twin)

    near_in(0)
    cross_in(0)
    cross_in(1)
    cross_in(3)
    near_in(1)
    near_in(3)
    near_in(2)
    cross_in(2)
    for d in (0, 1, 3, 2):
        got = of(x_hi, 1 - core, d)
        remote(got, got, c_send.at[d], c_recv.at[d], twin).wait_recv()
    for d in (0, 1, 3, 2):
        got = of(1 - x_hi, 1 - core, d)
        remote(got, got, c_send.at[4 + d], c_recv.at[4 + d], twin).wait_recv()

    @pl.when(jnp.logical_not(stays))
    def _():
        here.wait_send()

    for copy in sent:
        copy.wait_send()


def give_back(attended):
    anywhere = pl.BlockSpec(memory_space=pl.ANY)
    dma = pltpu.SemaphoreType.DMA
    return pl.pallas_call(
        return_kernel,
        out_shape=jax.ShapeDtypeStruct((16, ROWS // 2, 128), BF16),
        in_specs=[anywhere],
        out_specs=anywhere,
        scratch_shapes=[dma((8,)), dma((8,)), dma((8,)), dma((8,))],
        compiler_params=pltpu.CompilerParams(collective_id=1, has_side_effects=True, vmem_limit_bytes=16 << 20),
        name="give_back",
    )(attended)


def mix_kernel(att_ref, w_ref, out_ref):
    w = w_ref[...]
    half = ROWS // 2
    for side in range(2):
        cols = slice(side * HEAD_DIM, (side + 1) * HEAD_DIM)
        a = jnp.concatenate([att_ref[g][:, cols] for g in range(16)], axis=1)
        out_ref[side * half : (side + 1) * half, :] = jnp.dot(a, w, preferred_element_type=F32).astype(BF16)


def mix(attended, w_cols):
    whole = pl.BlockSpec(memory_space=pltpu.VMEM)
    return pl.pallas_call(
        mix_kernel,
        out_shape=jax.ShapeDtypeStruct((ROWS, 256), BF16),
        in_specs=[whole, whole],
        out_specs=whole,
        compiler_params=pltpu.CompilerParams(vmem_limit_bytes=16 << 20),
        name="mix",
    )(attended, w_cols)


def body(tokens, w_query, w_key, w_value, w_out, block_mask, block_order):
    kv, ones_v, w_all, lists, qz = exchange(
        tokens, w_query, w_key, w_value, w_out, block_mask, block_order.reshape(1, NB)
    )
    attended = attend(lists, kv.reshape(32 * ROWS, 128), ones_v, qz)
    everything = give_back(attended)
    return mix(everything, w_all.reshape(1024, 256))


def solution(mesh):
    placed = (P("ctx", None), P(None, "head"), P(None, "head"), P(None, "head"), P("head", None), P(), P())
    return jax.shard_map(body, mesh=mesh, in_specs=placed, out_specs=P("ctx", "head"), check_vma=False)
```

```python
import functools

import jax
import jax.numpy as jnp
from jax import lax
from jax.experimental import pallas as pl
from jax.experimental.pallas import tpu as pltpu
from jax.sharding import PartitionSpec as P

HEAD_DIM = 64
BLOCK = 128
NB = 128
ROWS = 512
NY, NZ = 4, 4
LIST_PAD = -1e30
MESH = pl.DeviceIdType.MESH
BF16 = jnp.bfloat16
F32 = jnp.float32


def place():
    ctx = lax.axis_index("ctx")
    head = lax.axis_index("head")
    return ctx // 8, (ctx // 2) % 4, ctx % 2, head // 2, head % 2


def ctx_of(y, z, x_lo):
    return (y * NZ + z) * 2 + x_lo


def write_lists(mask, order_row, z, core, lists_ref):
    sub = lax.broadcasted_iota(jnp.int32, (NB, NB), 0)
    lane = lax.broadcasted_iota(jnp.int32, (NB, NB), 1)
    nt = (((1,), (1,)), ((), ()))

    def as_bf16(condition):
        return condition.astype(F32).astype(BF16)

    initial_of = as_bf16(order_row == sub)
    mine = ((sub // 4 * NZ + z) * 2 + core) * 4 + sub % 4
    row_pick = as_bf16(jnp.logical_and(lane == mine, sub < 16))
    rows_initial = lax.dot_general(row_pick, initial_of, nt, preferred_element_type=F32).astype(BF16)
    mask_rows = jnp.dot(rows_initial, mask.astype(F32).astype(BF16), preferred_element_type=F32).astype(BF16)
    allowed = jnp.dot(mask_rows, initial_of, preferred_element_type=F32)
    rank = jnp.dot(allowed.astype(BF16), as_bf16(sub < lane), preferred_element_type=F32)
    rank = jnp.where(allowed > 0.5, rank, -1.0)
    sub_f = sub.astype(F32)
    lane_row = lax.broadcasted_iota(jnp.int32, (8, NB), 1).astype(F32).astype(BF16)
    for i in range(16):
        hot = as_bf16(rank[i : i + 1, :] == sub_f)
        got = lax.dot_general(lane_row, hot, nt, preferred_element_type=F32)
        lists_ref[i : i + 1, :] = got[0:1, :].astype(jnp.int32)
    ones = jnp.ones((8, NB), BF16)
    count = lax.dot_general(ones, allowed.astype(BF16), nt, preferred_element_type=F32)
    steps = jnp.floor((count + 1.0) * 0.5)
    total = jnp.sum(steps, axis=1, keepdims=True)
    counts = jnp.where(lane[0:8] == 32, total, count).astype(jnp.int32)
    lists_ref[16:32, :] = jnp.zeros((16, NB), jnp.int32)
    lists_ref[17:18, :] = counts[0:1]


def query_place(i):
    b = i % 4
    return i // 4, slice(b % 2 * BLOCK, (b % 2 + 1) * BLOCK), slice(b // 2 * HEAD_DIM, (b // 2 + 1) * HEAD_DIM)


def exchange_kernel(tok_hbm, wq_hbm, wk_hbm, wv_hbm, w_ref, mask_hbm, order_hbm,
                    kv_all, ones_v, w_all, lists_ref, qz,
                    tok_ref, wq_ref, wk_ref, wv_ref, mask_ref, order_ref, kv_ref, q_ref, q_all, in_sems,
                    a_send, a_recv, q_send, q_recv, w_send, w_recv, z_send, z_recv, c_send, c_recv):
    loads = [
        pltpu.make_async_copy(src, dst, in_sems.at[n])
        for n, (src, dst) in enumerate(
            [(wk_hbm, wk_ref), (tok_hbm, tok_ref), (wv_hbm, wv_ref), (wq_hbm, wq_ref), (mask_hbm, mask_ref), (order_hbm, order_ref)]
        )
    ]
    for load in loads:
        load.start()
    y, z, x_lo, x_hi, core = place()
    me_ctx = ctx_of(y, z, x_lo)
    me_head = x_hi * 2 + core
    swap_head = x_hi * 2 + x_lo
    stays = x_lo == core
    up = (ctx_of(y, (z + 1) % NZ, x_lo), me_head)
    down = (ctx_of(y, (z + 3) % NZ, x_lo), me_head)
    twin = (me_ctx, x_hi * 2 + 1 - core)
    head_peers = [(me_ctx, (me_head + k) % 4) for k in range(1, 4)]
    a_to = [(ctx_of((y + d) % NY, z, core), swap_head) for d in range(4)]

    barrier = pltpu.get_barrier_semaphore()
    for peer in [up, down, *head_peers, *a_to[1:]]:
        pl.semaphore_signal(barrier, inc=1, device_id=peer, device_id_type=MESH)

    @pl.when(jnp.logical_not(stays))
    def _():
        pl.semaphore_signal(barrier, inc=1, device_id=a_to[0], device_id_type=MESH)

    half = ROWS // 2
    columns = [slice(j * HEAD_DIM, (j + 1) * HEAD_DIM) for j in range(4)]
    loads[0].wait()
    loads[1].wait()
    tok = tok_ref[...]
    keys = jnp.dot(tok, wk_ref[...], preferred_element_type=F32).astype(BF16)
    loads[2].wait()
    vals = jnp.dot(tok, wv_ref[...], preferred_element_type=F32).astype(BF16)
    for j in range(4):
        kv_ref[j] = jnp.concatenate([keys[:, columns[j]], vals[:, columns[j]]], axis=1)

    pl.semaphore_wait(barrier, 8 + (x_lo + core) % 2)

    def remote(src, dst, send_sem, recv_sem, device):
        return pltpu.make_async_remote_copy(
            src_ref=src, dst_ref=dst, send_sem=send_sem, recv_sem=recv_sem, device_id=device, device_id_type=MESH
        )

    sent = []

    def send(src, dst, send_sem, recv_sem, device):
        copy = remote(src, dst, send_sem, recv_sem, device)
        copy.start()
        sent.append(copy)

    def arrived(dst, send_sem, recv_sem, device):
        remote(dst, dst, send_sem, recv_sem, device).wait_recv()

    own = y % NY
    kv_here = remote(kv_ref.at[own], kv_all.at[me_ctx], a_send.at[0], a_recv.at[0], a_to[0])
    q_here = remote(q_ref.at[own], q_all.at[y], q_send.at[0], q_recv.at[0], a_to[0])
    kv_local = pltpu.make_async_copy(kv_ref.at[own], kv_all.at[me_ctx], a_recv.at[0])
    q_local = pltpu.make_async_copy(q_ref.at[own], q_all.at[y], q_recv.at[0])

    def send_kv(d):
        send(kv_ref.at[(y + d) % NY], kv_all.at[me_ctx], a_send.at[d], a_recv.at[d], a_to[d])

    def send_q(d):
        send(q_ref.at[(y + d) % NY], q_all.at[y], q_send.at[d], q_recv.at[d], a_to[d])

    def chunk(d, dz):
        return kv_all.at[ctx_of((y + NY - d) % NY, (z + NZ + dz) % NZ, core)]

    def pass_on(d):
        send(chunk(d, 0), chunk(d, 0), z_send.at[d], z_recv.at[d], up)
        send(chunk(d, 0), chunk(d, 0), z_send.at[4 + d], z_recv.at[4 + d], down)
        send(chunk(d, 0), chunk(d, 0), c_send.at[d], c_recv.at[d], twin)

    def from_near(d):
        below, above = chunk(d, -1), chunk(d, 1)
        arrived(below, z_send.at[d], z_recv.at[d], up)
        if d in (0, 1):
            send(below, below, z_send.at[8 + d], z_recv.at[8 + d], up)
        send(below, below, c_send.at[4 + d], c_recv.at[4 + d], twin)
        arrived(above, z_send.at[4 + d], z_recv.at[4 + d], down)
        if d in (2, 3):
            send(above, above, z_send.at[8 + d], z_recv.at[8 + d], down)
        send(above, above, c_send.at[8 + d], c_recv.at[8 + d], twin)

    order = (1, 3, 2)
    onward = [(z_send.at[0], z_recv.at[0], up), (z_send.at[4], z_recv.at[4], down), (c_send.at[0], c_recv.at[0], twin)]

    @pl.when(stays)
    def _():
        for send_sem, recv_sem, device in onward:
            remote(kv_ref.at[own], kv_all.at[me_ctx], send_sem, recv_sem, device).start()
        kv_local.start()

    @pl.when(jnp.logical_not(stays))
    def _():
        kv_here.start()

    send_kv(1)
    send_kv(3)
    send_kv(2)

    @pl.when(jnp.logical_not(stays))
    def _():
        kv_here.wait_recv()
        for send_sem, recv_sem, device in onward:
            remote(chunk(0, 0), chunk(0, 0), send_sem, recv_sem, device).start()

    for send_sem, recv_sem, device in onward:
        sent.append(remote(chunk(0, 0), chunk(0, 0), send_sem, recv_sem, device))
    loads[3].wait()
    query = jnp.dot(tok, wq_ref[...], preferred_element_type=F32).astype(BF16)
    for j in range(4):
        q_ref[j] = jnp.concatenate([query[:half, columns[j]], query[half:, columns[j]]], axis=1)

    @pl.when(stays)
    def _():
        q_local.start()

    @pl.when(jnp.logical_not(stays))
    def _():
        q_here.start()

    for d in order:
        send_q(d)
    arrived(chunk(1, 0), a_send.at[1], a_recv.at[1], a_to[1])
    pass_on(1)
    arrived(chunk(3, 0), a_send.at[3], a_recv.at[3], a_to[3])
    pass_on(3)
    arrived(chunk(2, 0), a_send.at[2], a_recv.at[2], a_to[2])
    pass_on(2)
    from_near(0)
    for k in range(1, 4):
        to = (me_head + k) % 4
        send(w_ref.at[:, pl.ds(pl.multiple_of(to * 256, 256), 256)], w_all.at[me_head], w_send.at[k - 1], w_recv.at[k - 1],
             head_peers[k - 1])
    w_local = pltpu.make_async_copy(
        w_ref.at[:, pl.ds(pl.multiple_of(me_head * 256, 256), 256)], w_all.at[me_head], w_recv.at[3]
    )
    w_local.start()
    from_near(1)
    loads[4].wait()
    loads[5].wait()
    write_lists(mask_ref[...], order_ref[...], z, core, lists_ref)

    def twin_arrived(d, dz, place_of):
        got = kv_all.at[ctx_of((y + NY - d) % NY, (z + NZ + dz) % NZ, 1 - core)]
        arrived(got, c_send.at[place_of + d], c_recv.at[place_of + d], twin)

    def lay_out(d, dz, sides=(0, 1)):
        for side in sides:
            ctx = ctx_of((y + NY - d) % NY, (z + NZ + dz) % NZ, side)
            for b in range(ROWS // BLOCK):
                got = kv_all[ctx, b * BLOCK : (b + 1) * BLOCK, :].astype(F32)
                ones_v[ctx * 4 + b, 16:80, :] = jnp.transpose(got)[HEAD_DIM:, :].astype(BF16)

    def ones_of(block, _):
        ones_v[block, 0:16, :] = jnp.ones((16, 128), BF16)
        return 0

    lax.fori_loop(0, NB, ones_of, 0)

    @pl.when(stays)
    def _():
        q_local.wait()
        kv_local.wait()

    @pl.when(jnp.logical_not(stays))
    def _():
        q_here.wait_recv()

    for d in order:
        arrived(q_all.at[(y + NY - d) % NY], q_send.at[d], q_recv.at[d], a_to[d])
    narrow = lax.broadcasted_iota(jnp.int32, (BLOCK, 128), 1) < HEAD_DIM
    for i in range(16):
        step, rows, cols = query_place(i)
        q = q_all[step, rows, :]
        if cols.start:
            q = jnp.concatenate([q[:, HEAD_DIM:], q[:, :HEAD_DIM]], axis=1)
        qz[i] = jnp.where(narrow, q, jnp.zeros_like(q))
    qz[16] = jnp.zeros((BLOCK, 128), BF16)
    from_near(3)
    from_near(2)
    for d in (0, 1, 3, 2):
        twin_arrived(d, 0, 0)
        lay_out(d, 0)
    for d in (0, 1, 3, 2):
        twin_arrived(d, -1, 4)
        twin_arrived(d, 1, 8)
        lay_out(d, -1)
        lay_out(d, 1)
        far = chunk(d, 2)
        arrived(far, z_send.at[8 + d], z_recv.at[8 + d], up)
        send(far, far, c_send.at[12 + d], c_recv.at[12 + d], twin)
    for d in (0, 1, 3, 2):
        lay_out(d, 2, (core,))
        twin_arrived(d, 2, 12)
        lay_out(d, 2, (1 - core,))

    @pl.when(jnp.logical_not(stays))
    def _():
        kv_here.wait_send()
        q_here.wait_send()

    for k in range(1, 4):
        arrived(w_all.at[(me_head + 4 - k) % 4], w_send.at[k - 1], w_recv.at[k - 1], head_peers[k - 1])
    w_local.wait()
    for copy in sent:
        copy.wait_send()


def exchange(tokens, w_query, w_key, w_value, w_out, block_mask, order_row):
    in_hbm = pl.BlockSpec(memory_space=pltpu.HBM)
    operands = [tokens, w_query, w_key, w_value, w_out, block_mask, order_row]
    operands = [pltpu.with_memory_space_constraint(a, pltpu.HBM) for a in operands]
    anywhere = pl.BlockSpec(memory_space=pl.ANY)
    dma = pltpu.SemaphoreType.DMA
    vmem = pltpu.VMEM
    in_vmem = pl.BlockSpec(memory_space=vmem)
    return pl.pallas_call(
        exchange_kernel,
        out_shape=(
            jax.ShapeDtypeStruct((32, ROWS, 128), BF16),
            jax.ShapeDtypeStruct((NB, 80, BLOCK), BF16),
            jax.ShapeDtypeStruct((4, 256, 256), BF16),
            jax.ShapeDtypeStruct((32, NB), jnp.int32),
            jax.ShapeDtypeStruct((17, BLOCK, 128), BF16),
        ),
        in_specs=[in_hbm] * 7,
        out_specs=(in_vmem, in_vmem, anywhere, in_vmem, in_vmem),
        scratch_shapes=[
            vmem((ROWS, 1024), BF16), vmem((1024, 256), BF16), vmem((1024, 256), BF16), vmem((1024, 256), BF16),
            vmem((NB, NB), jnp.int32), vmem((1, NB), jnp.int32), vmem((4, ROWS, 128), BF16), vmem((4, ROWS // 2, 128), BF16),
            vmem((4, ROWS // 2, 128), BF16), dma((6,)),
            dma((4,)), dma((4,)), dma((4,)), dma((4,)), dma((4,)), dma((4,)),
            dma((12,)), dma((12,)), dma((16,)), dma((16,)),
        ],
        compiler_params=pltpu.CompilerParams(collective_id=0, has_side_effects=True, vmem_limit_bytes=24 << 20),
        name="exchange",
    )(*operands)


UNROLL = 7
EXP2_SCALE = (HEAD_DIM ** -0.5) * 1.4426950408889634
SMALLEST, LARGEST = 1e-20, 1e30
NT = (((1,), (1,)), ((), ()))


def attend_kernel(lists, kv_ref, ones_v, qz, out_ref, acc, sbuf, scores):
    zero = jnp.zeros((BLOCK, 128), F32)
    for i in range(17):
        acc[i] = jnp.zeros((80, BLOCK), F32)
    second = lax.broadcasted_iota(jnp.int32, (2 * BLOCK, 1), 0) >= BLOCK

    def block_at(i, k):
        return lists[i, jnp.minimum(k, NB - 1)]

    def rows_at(i, k):
        return pl.ds(pl.multiple_of(block_at(i, k) * BLOCK, BLOCK), BLOCK)

    def advance(i, k):
        done = k + 2 >= lists[17, i]
        return jnp.minimum(jnp.where(done, i + 1, i), 16), jnp.where(done, 0, k + 2)

    def score(slot, i, k):
        for u in range(UNROLL):
            keys = jnp.concatenate([kv_ref[rows_at(i, k), :], kv_ref[rows_at(i, k + 1), :]], axis=0)
            bias = jnp.where(k + 1 < lists[17, i], 0.0, LIST_PAD).astype(F32)
            s = lax.dot_general(keys, qz[i], NT, preferred_element_type=F32)
            sbuf[slot, u] = jnp.exp2(s * EXP2_SCALE + jnp.where(second, bias, 0.0)).astype(BF16)
            i, k = advance(i, k)
        return i, k

    def weigh(slot, i, k):
        for u in range(UNROLL):
            vals = jnp.concatenate([ones_v[block_at(i, k)], ones_v[block_at(i, k + 1)]], axis=1)
            acc[i] += jnp.dot(vals, sbuf[slot, u], preferred_element_type=F32)
            i, k = advance(i, k)

    start = jnp.int32(0)
    i1, k1 = score(0, start, start)

    def step(_, carry):
        i, k, i1, k1 = carry
        i2, k2 = score(1, i1, k1)
        weigh(0, i, k)
        i3, k3 = score(0, i2, k2)
        weigh(1, i1, k1)
        return i2, k2, i3, k3

    lax.fori_loop(0, (lists[17, 32] + 2 * UNROLL - 1) // (2 * UNROLL), step, (start, start, i1, k1))

    fine = jnp.full((1, BLOCK), 1.0, F32)
    for i in range(16):
        y, rows, cols = query_place(i)
        denom = acc[i][0:1, :]
        within = jnp.logical_and(denom >= SMALLEST, denom <= LARGEST)
        fine = jnp.where(within, fine, 0.0)
        out_ref[y, rows, cols] = jnp.transpose(acc[i][16:80, :] / denom).astype(BF16)

    @pl.when(jnp.min(fine) < 0.5)
    def _():
        for i in range(16):
            y, rows, cols = query_place(i)
            n = lists[17, i]

            def first(k, top):
                s = lax.dot_general(qz[i], kv_ref[rows_at(i, k), :], NT, preferred_element_type=F32)
                scores[k] = s
                return jnp.maximum(top, s)

            top = lax.fori_loop(0, n, first, jnp.full((BLOCK, BLOCK), -3e38, F32))
            top = jnp.max(top, axis=1, keepdims=True)

            def then(k, carry):
                total, weighted = carry
                p = jnp.exp2((scores[k] - top) * EXP2_SCALE)
                return total + p, weighted + jnp.dot(
                    p.astype(BF16), kv_ref[rows_at(i, k), :], preferred_element_type=F32
                )

            total, weighted = lax.fori_loop(0, n, then, (zero, zero))
            denom = jnp.sum(total, axis=1, keepdims=True)
            out_ref[y, rows, cols] = (weighted[:, HEAD_DIM:] / denom).astype(BF16)


def attend(lists, kv, ones_v, qz):
    whole = pl.BlockSpec(memory_space=pltpu.VMEM)
    vmem = pltpu.VMEM
    return pl.pallas_call(
        attend_kernel,
        out_shape=jax.ShapeDtypeStruct((4, ROWS // 2, 128), BF16),
        grid_spec=pltpu.PrefetchScalarGridSpec(
            num_scalar_prefetch=1,
            grid=(),
            in_specs=[whole] * 3,
            out_specs=whole,
            scratch_shapes=[
                vmem((17, 80, BLOCK), F32),
                vmem((2, UNROLL, 2 * BLOCK, BLOCK), BF16),
                vmem((NB, BLOCK, BLOCK), F32),
            ],
        ),
        compiler_params=pltpu.CompilerParams(vmem_limit_bytes=24 << 20),
        name="attend",
    )(lists, kv, ones_v, qz)


def return_kernel(att_ref, all_ref, send_sems, recv_sems, c_send, c_recv):
    y, z, x_lo, x_hi, core = place()
    me_ctx = ctx_of(y, z, x_lo)
    stays = x_lo == core
    twin = (me_ctx, x_hi * 2 + 1 - core)
    me_global = (x_hi * 2 + x_lo) * 4 + y
    near = [(ctx_of((y + d) % NY, z, core), x_hi * 2 + x_lo) for d in range(4)]
    cross = [(ctx_of((y + d) % NY, z, core), (1 - x_hi) * 2 + x_lo) for d in range(4)]

    barrier = pltpu.get_barrier_semaphore()
    for peer in [twin, *cross, *near[1:]]:
        pl.semaphore_signal(barrier, inc=1, device_id=peer, device_id_type=MESH)

    @pl.when(jnp.logical_not(stays))
    def _():
        pl.semaphore_signal(barrier, inc=1, device_id=near[0], device_id_type=MESH)

    pl.semaphore_wait(barrier, 8 + (x_lo + core) % 2)

    def remote(src, dst, send_sem, recv_sem, device):
        return pltpu.make_async_remote_copy(
            src_ref=src, dst_ref=dst, send_sem=send_sem, recv_sem=recv_sem, device_id=device, device_id_type=MESH
        )

    sent = []

    def send(src, dst, send_sem, recv_sem, device):
        copy = remote(src, dst, send_sem, recv_sem, device)
        copy.start()
        sent.append(copy)

    def send_near(d):
        send(att_ref.at[(y + d) % NY], all_ref.at[me_global], send_sems.at[d], recv_sems.at[d], near[d])

    def send_cross(d):
        send(att_ref.at[(y + d) % NY], all_ref.at[me_global], send_sems.at[4 + d], recv_sems.at[4 + d], cross[d])

    here = remote(att_ref.at[y], all_ref.at[me_global], send_sems.at[0], recv_sems.at[0], near[0])
    local = pltpu.make_async_copy(att_ref.at[y], all_ref.at[me_global], recv_sems.at[0])
    send_cross(2)
    send_cross(1)
    send_cross(3)
    send_near(2)
    send_cross(0)
    send_near(1)
    send_near(3)

    @pl.when(stays)
    def _():
        local.start()

    @pl.when(jnp.logical_not(stays))
    def _():
        here.start()

    def of(source_hi, source_lo, d):
        return all_ref.at[(source_hi * 2 + source_lo) * 4 + (y + NY - d) % NY]

    def near_in(d):
        got = of(x_hi, core, d)
        if d == 0:
            @pl.when(stays)
            def _():
                local.wait()

            @pl.when(jnp.logical_not(stays))
            def _():
                here.wait_recv()
        else:
            remote(got, got, send_sems.at[d], recv_sems.at[d], near[d]).wait_recv()
        send(got, got, c_send.at[d], c_recv.at[d], twin)

    def cross_in(d):
        got = of(1 - x_hi, core, d)
        remote(got, got, send_sems.at[4 + d], recv_sems.at[4 + d], cross[d]).wait_recv()
        send(got, got, c_send.at[4 + d], c_recv.at[4 + d], twin)

    near_in(0)
    cross_in(0)
    cross_in(1)
    cross_in(3)
    near_in(1)
    near_in(3)
    near_in(2)
    cross_in(2)
    for d in (0, 1, 3, 2):
        got = of(x_hi, 1 - core, d)
        remote(got, got, c_send.at[d], c_recv.at[d], twin).wait_recv()
    for d in (0, 1, 3, 2):
        got = of(1 - x_hi, 1 - core, d)
        remote(got, got, c_send.at[4 + d], c_recv.at[4 + d], twin).wait_recv()

    @pl.when(jnp.logical_not(stays))
    def _():
        here.wait_send()

    for copy in sent:
        copy.wait_send()


def give_back(attended):
    anywhere = pl.BlockSpec(memory_space=pl.ANY)
    dma = pltpu.SemaphoreType.DMA
    return pl.pallas_call(
        return_kernel,
        out_shape=jax.ShapeDtypeStruct((16, ROWS // 2, 128), BF16),
        in_specs=[anywhere],
        out_specs=anywhere,
        scratch_shapes=[dma((8,)), dma((8,)), dma((8,)), dma((8,))],
        compiler_params=pltpu.CompilerParams(collective_id=1, has_side_effects=True, vmem_limit_bytes=16 << 20),
        name="give_back",
    )(attended)


def mix_kernel(att_ref, w_ref, out_ref, made, sems):
    stores = []
    w = w_ref[...]
    half = ROWS // 2
    for side in range(2):
        cols = slice(side * HEAD_DIM, (side + 1) * HEAD_DIM)
        a = jnp.concatenate([att_ref[g][:, cols] for g in range(16)], axis=1)
        rows = slice(side * half, (side + 1) * half)
        made[rows, :] = jnp.dot(a, w, preferred_element_type=F32).astype(BF16)
        stores.append(pltpu.make_async_copy(made.at[rows], out_ref.at[rows], sems.at[side]))
        stores[-1].start()
    for store in stores:
        store.wait()


def mix(attended, w_cols):
    whole = pl.BlockSpec(memory_space=pltpu.VMEM)
    return pl.pallas_call(
        mix_kernel,
        out_shape=jax.ShapeDtypeStruct((ROWS, 256), BF16),
        in_specs=[whole, whole],
        out_specs=pl.BlockSpec(memory_space=pl.ANY),
        scratch_shapes=[pltpu.VMEM((ROWS, 256), BF16), pltpu.SemaphoreType.DMA((2,))],
        compiler_params=pltpu.CompilerParams(vmem_limit_bytes=16 << 20),
        name="mix",
    )(attended, w_cols)


def body(tokens, w_query, w_key, w_value, w_out, block_mask, block_order):
    kv, ones_v, w_all, lists, qz = exchange(
        tokens, w_query, w_key, w_value, w_out, block_mask, block_order.reshape(1, NB)
    )
    attended = attend(lists, kv.reshape(32 * ROWS, 128), ones_v, qz)
    everything = give_back(attended)
    return mix(everything, w_all.reshape(1024, 256))


def solution(mesh):
    placed = (P("ctx", None), P(None, "head"), P(None, "head"), P(None, "head"), P("head", None), P(), P())
    return jax.shard_map(body, mesh=mesh, in_specs=placed, out_specs=P("ctx", "head"), check_vma=False)
```
